512 devices in a mesh: seq: 128 (over y, z, core), tp: 4 (over x).
Axes of the slice: x: 4, y: 4, z: 16, core: 2. Of those that a mesh axis runs over, the one named last changes fastest.
Arguments:
- layer_input: bfloat16 [16384, 1600], P(('seq', 'tp')), may hold values from -6 to 6
- out_grad: bfloat16 [16384, 1600], P(('seq', 'tp')), may hold values from -2.5 to 2.5
- w_in: bfloat16 [1600, 1600], P('tp'), may hold values from -0.15625 to 0.15625
- w_gate: bfloat16 [1600, 1600], P('tp'), may hold values from -0.15625 to 0.15625
- w_out: bfloat16 [1600, 1600], P('tp'), may hold values from -0.15625 to 0.15625
- b_proj: bfloat16 [16, 16384], P(None, 'seq'), may hold values from -3 to 3
- c_proj: bfloat16 [16, 16384], P(None, 'seq'), may hold values from -3 to 3
- log_decay: bfloat16 [25, 16384], P(None, 'seq'), may hold values from -1 to 0
- d_skip: float32 [1600], P('tp'), may hold values from 0.5 to 1.5
- entry_state: float32 [16, 1600], P(None, 'tp'), may hold values from -6 to 6
- doc_start: int32 [16384], P('seq'), may hold values 0 or 1
Outputs:
- input_grad: bfloat16 [16384, 1600], P(('seq', 'tp'))
- b_grad: float32 [16, 16384], P(None, 'seq')
- c_grad: float32 [16, 16384], P(None, 'seq')
The draws below stay inside these ranges and needn't reach their ends.
All inputs are finite; a program needn't handle non-finite values. No bound on the sum of `doc_start` on one device may be relied on, other than what follows from the above.
Results may differ from the reference program's by a relative error of at most 0.0065.
Values may be sent and summed in bfloat16 or wider, within the bound.
A program may use at most 128 MiB of HBM per device.

```python
import math
import jax
import jax.numpy as jnp
from jax import lax

D = 1600
STATE = 16
RECURRENT_HEADS = 25
HDIM = 64
TOK_DEV = 128
TOKENS = 16384
INNER = 1600


def draw_log_decay(key, part):
    key = jax.random.fold_in(key, 7)
    random_subkeys = jax.random.split(key, 5)
    shape_power = 1.0
    slowest = 0.5 / TOKENS
    fastest = 1.0 / 30.0
    picked = jax.random.uniform(random_subkeys[0], (RECURRENT_HEADS,), jnp.float32) ** shape_power
    step_rates = jnp.exp(math.log(slowest) + (math.log(fastest) - math.log(slowest)) * picked)
    spread = math.log(2.0)
    roughness = jnp.exp(jax.random.uniform(random_subkeys[1], (RECURRENT_HEADS, TOKENS), jnp.float32, -spread, spread))
    device_part = jnp.exp(jax.random.uniform(random_subkeys[2], (RECURRENT_HEADS, TOKENS // TOK_DEV, 1), jnp.float32, -spread, spread))
    device_part = jnp.broadcast_to(device_part, (RECURRENT_HEADS, TOKENS // TOK_DEV, TOK_DEV)).reshape(RECURRENT_HEADS, TOKENS)
    rate_logarithms = -step_rates[:, None] * roughness * device_part
    fourth_part = TOKENS // 4
    sudden_rows = jnp.arange(4, dtype=jnp.int32)[None, :] * fourth_part + jax.random.randint(random_subkeys[3], (RECURRENT_HEADS, 4), 0, fourth_part)
    loss_values = jax.random.uniform(random_subkeys[4], (RECURRENT_HEADS, 4), jnp.float32, 0.2, 0.5)
    rows_per_head = jnp.broadcast_to(jnp.arange(RECURRENT_HEADS, dtype=jnp.int32)[:, None], (RECURRENT_HEADS, 4))
    rate_logarithms = rate_logarithms.at[rows_per_head, sudden_rows].add(jnp.log1p(-loss_values))
    return rate_logarithms.astype(jnp.bfloat16)


def touch_ends(values, rng, low, top_value):
    longest = values.shape.index(max(values.shape))
    spots = []
    for shift in (0, 1):
        where = [jax.random.randint(jax.random.fold_in(rng, axis), (), 0, length) for axis, length in enumerate(values.shape)]
        where[longest] = (where[longest] + shift) % values.shape[longest]
        spots.append(tuple(where))
    return values.at[spots[0]].set(low).at[spots[1]].set(top_value)


def block_levels(own_key, shape, cuts, smallest, high):
    factor_of, own = 1.0, jax.random.fold_in(own_key, 6)
    for axis_at, parts in cuts:
        steps = jnp.exp(jax.random.uniform(jax.random.fold_in(own, axis_at), (parts,), jnp.float32, smallest / len(cuts), high / len(cuts)))
        factor_of = factor_of * jnp.repeat(steps, shape[axis_at] // parts).reshape([-1 if axis == axis_at else 1 for axis in range(len(shape))])
    return factor_of


def normal_values(stream_key, shape, scale, bound, cuts=(), held_as=jnp.bfloat16):
    array = scale * jax.random.normal(stream_key, shape, jnp.float32)
    if cuts:
        array = array * block_levels(stream_key, shape, cuts, -0.22, 0.18)
    return jnp.clip(array, -bound, bound).astype(held_as)


def setup_inputs(seed: int = 0) -> dict:
    seeds = jax.random.split(jax.random.key(seed), 12)
    return {
        "layer_input": normal_values(seeds[0], (TOKENS, D), 1.0, 6.0, ((0, 512),)),
        "out_grad": normal_values(seeds[1], (TOKENS, D), 0.3, 2.5, ((0, 512),)),
        "w_in": normal_values(seeds[2], (INNER, D), D ** -0.5, 0.15625, ((0, 4),)),
        "w_gate": normal_values(seeds[3], (INNER, D), D ** -0.5, 0.15625, ((0, 4),)),
        "w_out": normal_values(seeds[4], (INNER, D), INNER ** -0.5, 0.15625, ((0, 4),)),
        "b_proj": normal_values(seeds[5], (STATE, TOKENS), 0.5, 3.0, ((1, 128),)),
        "c_proj": normal_values(seeds[6], (STATE, TOKENS), 0.5, 3.0, ((1, 128),)),
        "log_decay": draw_log_decay(jax.random.fold_in(seeds[11], 71), 0),
        "d_skip": jnp.clip(0.5 + 1.0 * jax.random.uniform(seeds[8], (INNER,), jnp.float32) ** block_levels(seeds[8], (INNER,), ((0, 4),), -0.2, 0.2), 0.5, 1.5),
        "entry_state": normal_values(seeds[9], (STATE, INNER), 1.0, 6.0, ((1, 4),), jnp.float32),
        "doc_start": touch_ends((jax.random.randint(seeds[10], (TOKENS,), 0, TOKENS // 8) < 1).astype(jnp.int32), jax.random.fold_in(seeds[10], 1), 0, 1),
    }


FULL_PRECISION = lax.Precision.HIGHEST

def silu_slope(values):
    logistic = jax.nn.sigmoid(values)
    return logistic * (1.0 + values * (1.0 - logistic))

def reference(layer_input, out_grad, w_in, w_gate, w_out, b_proj, c_proj, log_decay, d_skip, entry_state, doc_start):
    pre_act = jnp.dot(layer_input, w_in.T, preferred_element_type=jnp.float32)
    gate_act = jnp.dot(layer_input, w_gate.T, preferred_element_type=jnp.float32)
    x_rows = jax.nn.silu(pre_act).astype(jnp.bfloat16)
    mix_grad = jnp.dot(out_grad, w_out.T, preferred_element_type=jnp.float32)
    y_grads = (mix_grad * jax.nn.silu(gate_act)).astype(jnp.bfloat16)
    log_keep = jnp.repeat(log_decay.astype(jnp.float32), HDIM, axis=0).T
    resets = jnp.concatenate([jnp.zeros((1,), jnp.int32), doc_start[1:].astype(jnp.int32)])
    fresh_rows = (resets == 1)[:, None]
    keep_rate = jnp.where(fresh_rows, 0.0, jnp.exp(log_keep)).astype(jnp.float32)
    input_scale = jnp.where(fresh_rows, 1.0, jnp.sqrt(-jnp.expm1(2.0 * log_keep))).astype(jnp.float32)
    inputs = x_rows.astype(jnp.float32) * input_scale
    grad_rows = y_grads.astype(jnp.float32)
    b_rows = b_proj.astype(jnp.float32).T
    c_rows = c_proj.astype(jnp.float32).T

    def forward(states, pieces):
        keep_t, input_t, b_t, c_t, grad_t = pieces
        states = keep_t[None, :] * states + b_t[:, None] * input_t[None, :]
        out_t = jnp.dot(c_t, states, precision=FULL_PRECISION)
        c_grad_t = jnp.dot(states, grad_t, precision=FULL_PRECISION)
        return (states, (out_t, c_grad_t))
    sequence = (keep_rate, inputs, b_rows, c_rows, grad_rows)
    start_state = entry_state.astype(jnp.float32)
    _, (ssm_part, c_grad) = lax.scan(forward, start_state, sequence)
    ssm_out = (ssm_part + d_skip[None, :] * x_rows.astype(jnp.float32)).astype(jnp.bfloat16)

    def backward(carried, pieces):
        keep_t, input_t, b_t, c_t, grad_t = pieces
        state_grad = c_t[:, None] * grad_t[None, :] + carried
        x_part_t = jnp.dot(b_t, state_grad, precision=FULL_PRECISION)
        b_grad_t = jnp.dot(state_grad, input_t, precision=FULL_PRECISION)
        return (keep_t[None, :] * state_grad, (x_part_t, b_grad_t))
    zero_state = jnp.zeros(entry_state.shape, jnp.float32)
    _, (x_part, b_grad) = lax.scan(backward, zero_state, sequence, reverse=True)
    x_grad = (x_part * input_scale + d_skip[None, :] * grad_rows).astype(jnp.bfloat16)
    pre_grad = (x_grad.astype(jnp.float32) * silu_slope(pre_act)).astype(jnp.bfloat16)
    gate_grad = (mix_grad * ssm_out.astype(jnp.float32) * silu_slope(gate_act)).astype(jnp.bfloat16)
    total_grad = jnp.dot(pre_grad, w_in, preferred_element_type=jnp.float32) + jnp.dot(gate_grad, w_gate, preferred_element_type=jnp.float32)
    return (total_grad.astype(jnp.bfloat16), b_grad.T, c_grad.T)
```

```python
import functools

import jax
import jax.numpy as jnp
from jax import lax
from jax.experimental import pallas as pl
from jax.experimental.pallas import tpu as pltpu
from jax.sharding import PartitionSpec as P

HDIM = 64
LANES = 128
MESH = pl.DeviceIdType.MESH
F32 = jnp.float32
BF16 = jnp.bfloat16
NN = (((1,), (0,)), ((), ()))
NT = (((1,), (1,)), ((), ()))
TN = (((0,), (0,)), ((), ()))
CHUNKS = ((0, 512), (512, 1024), (1024, 1600))


def dot(a, b, dims):
    return lax.dot_general(a, b, dims, preferred_element_type=F32)


def parts(value, count):
    high = value.astype(BF16)
    if count == 1:
        return (high,)
    return (high, (value - high.astype(F32)).astype(BF16))


def mm(a, b, dims):
    total = None
    for i, left in enumerate(a):
        for j, right in enumerate(b):
            if i + j < 2:
                term = dot(left, right, dims)
                total = term if total is None else total + term
    return total


def one_minus_exp(u):
    series = 1.0 - u / 6.0
    for k in (5.0, 4.0, 3.0, 2.0):
        series = 1.0 - u / k * series
    return jnp.where(u < 0.25, u * series, 1.0 - jnp.exp(-u))


def kernel(
    row_len,
    groups,
    ways,
    x_hbm,
    g_hbm,
    wi_hbm,
    wg_hbm,
    wo_hbm,
    b_ref,
    c_ref,
    log_ref,
    skip_ref,
    entry_ref,
    doc_ref,
    out_ref,
    bg_ref,
    cg_ref,
    xbuf,
    gbuf,
    wi,
    wg,
    wo,
    entry_t,
    f_send,
    f_recv,
    f_pre,
    fy_buf,
    p_send,
    p_recv,
    res,
    land,
    t_buf,
    wide,
    bc_buf,
    rs_send,
    rs_recv,
    lsem,
    gs,
    gr,
    fs,
    fr,
    ys,
    yr,
    ps,
    pr,
    ts,
    tr,
    ss,
    sr,
    bs,
    br,
    rs,
    rr,
):
    me = lax.axis_index("seq")
    tp = lax.axis_index("tp")
    group = lax.div(me, row_len)
    rank = lax.rem(me, row_len)
    unit = lax.div(rank, 2)
    way = lax.rem(rank, 2)
    block = x_hbm.shape[0]
    tokens = ways * block
    channels = wi_hbm.shape[0]
    heads = log_ref.shape[0]
    state = b_ref.shape[0]
    tiles = p_recv.shape[1]
    spans = [(k, k * LANES, min(channels, (k + 1) * LANES)) for k in range(tiles)]

    local = [
        pltpu.make_async_copy(wi_hbm, wi, lsem.at[0]),
        pltpu.make_async_copy(wg_hbm, wg, lsem.at[1]),
        pltpu.make_async_copy(wo_hbm, wo, lsem.at[2]),
        pltpu.make_async_copy(x_hbm, xbuf.at[tp], lsem.at[3]),
        pltpu.make_async_copy(g_hbm, gbuf.at[tp], lsem.at[4]),
    ]
    for copy in local:
        copy.start()

    def row_peer(i):
        return group * row_len + lax.rem(rank + i, row_len)

    def group_peer(k):
        return lax.rem(group + k, groups) * row_len + rank

    def way_peer(k):
        return lax.rem(tp + k, ways)

    barrier = pltpu.get_barrier_semaphore()

    def greet(i, carry):
        pl.semaphore_signal(barrier, inc=1, device_id=(row_peer(i), tp), device_id_type=MESH)
        return carry

    lax.fori_loop(1, row_len, greet, 0)
    for k in range(1, groups):
        pl.semaphore_signal(barrier, inc=1, device_id=(group_peer(k), tp), device_id_type=MESH)
    for k in range(1, ways):
        pl.semaphore_signal(barrier, inc=1, device_id=(me, way_peer(k)), device_id_type=MESH)
    pl.semaphore_wait(barrier, row_len + groups + ways - 3)

    gathers = []
    for a, (src, dst) in enumerate(((x_hbm, xbuf), (g_hbm, gbuf))):
        for k in range(1, ways):
            copy = pltpu.make_async_remote_copy(
                src_ref=src,
                dst_ref=dst.at[tp],
                send_sem=gs.at[a, k - 1],
                recv_sem=gr.at[a, k - 1],
                device_id=(me, way_peer(k)),
                device_id_type=MESH,
            )
            copy.start()
            gathers.append(copy)

    def to_row(src_at, dst, send_sem, recv_sem):
        def send(i, carry):
            pltpu.make_async_remote_copy(
                src_ref=src_at(lax.rem(rank + i, row_len)),
                dst_ref=dst,
                send_sem=send_sem,
                recv_sem=recv_sem,
                device_id=(row_peer(i), tp),
                device_id_type=MESH,
            ).start()
            return carry

        lax.fori_loop(1, row_len, send, 0)

    def to_groups(buf, send_sem, recv_sem):
        copies = []
        for k in range(1, groups):
            copy = pltpu.make_async_remote_copy(
                src_ref=buf.at[group],
                dst_ref=buf.at[group],
                send_sem=send_sem.at[k - 1],
                recv_sem=recv_sem.at[k - 1],
                device_id=(group_peer(k), tp),
                device_id_type=MESH,
            )
            copy.start()
            copies.append(copy)
        return copies

    def wait_row(sem):
        every = p_recv.at[pl.ds(0, row_len - 1)]
        pltpu.make_async_copy(every, every, sem).wait()

    head_row = lax.broadcasted_iota(jnp.int32, (heads, channels), 0)
    chan_row = lax.broadcasted_iota(jnp.int32, (heads, channels), 1) + tp * channels
    low = head_row * HDIM
    pick = jnp.where((chan_row >= low) & (chan_row < low + HDIM), 1.0, 0.0).astype(BF16)
    logs = dot(log_ref[...], pick, TN)
    row_at = lax.broadcasted_iota(jnp.int32, (tokens, tokens), 0)
    col_at = lax.broadcasted_iota(jnp.int32, (tokens, tokens), 1)
    tri = jnp.where(row_at >= col_at, 1.0, 0.0).astype(BF16)
    eye = jnp.where(row_at == col_at, 1.0, 0.0).astype(BF16)
    cumulative = dot(tri, logs.astype(BF16), NN)
    at = lax.broadcasted_iota(jnp.int32, (1, tokens), 1) + me
    marks = jnp.where(at > 0, doc_ref[...], 0).astype(F32)
    marks_wide = jnp.broadcast_to(marks, (channels, tokens)).astype(BF16)
    marks_sq = jnp.broadcast_to(marks, (tokens, tokens)).astype(BF16)
    counts = dot(tri, marks_wide, NT)
    mark_col = dot(eye, marks_wide, NT)
    counts_col = dot(tri, marks_sq, NT)
    counts_row = dot(marks_sq, tri, NT)
    last = counts[tokens - 1 : tokens, :]
    total = cumulative[tokens - 1 : tokens, :]
    factor = jnp.where(last == 0.0, jnp.exp(total), 0.0)

    f_send[...] = jnp.zeros_like(f_send)
    for k, lo, hi in spans:
        f_send[k : k + 1, 0 : hi - lo] = factor[:, lo:hi]
    f_recv[rank] = f_send[...]
    to_row(lambda peer: f_send, f_recv.at[rank], fs, fr)

    p_send[...] = jnp.zeros_like(p_send)
    entry_t[...] = jnp.zeros_like(entry_t)
    entry = entry_ref[...]
    for k, lo, hi in spans:
        entry_t[:, k, 0 : hi - lo] = entry[:, lo:hi]

    scales = jnp.where(mark_col == 1.0, 1.0, jnp.sqrt(one_minus_exp(-2.0 * logs)))
    centre = cumulative[tokens // 2 : tokens // 2 + 1, :]
    rising = jnp.exp(cumulative - centre)
    falling = jnp.exp(centre - cumulative)
    carry_in = jnp.where(counts == 0.0, jnp.exp(cumulative), 0.0)
    carry_out = jnp.where(counts == last, jnp.exp(total - cumulative), 0.0)
    causal = (row_at >= col_at) & (counts_col == counts_row)
    b_rows = b_ref[...]
    c_rows = c_ref[...]
    crossed = jnp.where(causal, dot(c_rows, b_rows, TN), 0.0)
    skip = skip_ref[...]

    wait_row(fr)

    def at_step(i, count):
        return jnp.where(way == 0, i, count - 1 - i)

    def decay_step(i, product):
        j = at_step(i, row_len)
        f_pre[j] = product
        return product * f_recv[j]

    fy_buf[group] = lax.fori_loop(0, row_len, decay_step, jnp.ones((tiles, LANES), F32))
    decay_copies = to_groups(fy_buf, ys, yr)

    for copy in gathers[: ways - 1]:
        copy.wait_recv()
    local[3].wait()
    local[0].wait()
    rows = xbuf[...].reshape(tokens, x_hbm.shape[1])
    pre_act = dot(rows, wi[...], NT)
    local[1].wait()
    gate_act = dot(rows, wg[...], NT)
    pre_sig = jax.nn.sigmoid(pre_act)
    gate_sig = jax.nn.sigmoid(gate_act)
    x_rows = (pre_act * pre_sig).astype(BF16).astype(F32)
    gate_silu = gate_act * gate_sig
    scaled = x_rows * scales
    scaled_out = parts(scaled * carry_out, 2)
    state_part = mm((b_rows,), scaled_out, NN)
    for k, lo, hi in spans:
        p_send[:, 0, k, 0 : hi - lo] = state_part[:, lo:hi]
    for copy in gathers[ways - 1 :]:
        copy.wait_recv()
    local[4].wait()
    local[2].wait()
    mix_grad = dot(gbuf[...].reshape(tokens, g_hbm.shape[1]), wo[...], NT)
    y_grads = (mix_grad * gate_silu).astype(BF16).astype(F32)
    grads_in = parts(y_grads * carry_in, 2)
    grad_part = mm((c_rows,), grads_in, NN)
    for k, lo, hi in spans:
        p_send[:, 1, k, 0 : hi - lo] = grad_part[:, lo:hi]

    p_recv[rank] = p_send[unit, way]
    to_row(lambda peer: p_send.at[lax.div(peer, 2), lax.rem(peer, 2)], p_recv.at[rank], ps, pr)

    upper = parts(y_grads * rising, 2)
    lower = parts(scaled * falling, 2)
    weight = parts(jnp.where(causal, mm(upper, lower, NT), 0.0), 2)
    crossed_parts = parts(crossed, 2)
    ssm_own = rising * mm(crossed_parts, lower, NN) + skip * x_rows
    x_own = falling * mm(crossed_parts, upper, TN)
    c_own = mm((b_rows,), weight, NT)
    b_own = mm((c_rows,), weight, NN)
    pre_slope = pre_sig * (1.0 + pre_act * (1.0 - pre_sig))
    gate_slope = mix_grad * (gate_sig * (1.0 + gate_act * (1.0 - gate_sig)))

    wait_row(pr)

    def scan_step(i, carried):
        j = at_step(i, row_len)
        res[j] = carried
        return f_recv[j] * carried + p_recv[j]

    t_buf[group] = lax.fori_loop(0, row_len, scan_step, jnp.zeros((tiles, LANES), F32))
    total_copies = to_groups(t_buf, ts, tr)
    for copy in decay_copies:
        copy.wait_recv()
    for copy in total_copies:
        copy.wait_recv()
    carried = jnp.where(way == 0, entry_t[unit], 0.0)
    ahead = at_step(group, groups)
    for i in range(groups):
        j = at_step(i, groups)
        carried = jnp.where(i < ahead, fy_buf[j] * carried + t_buf[j], carried)
    res[...] = res[...] + f_pre[...] * carried[None]
    land[unit, way] = res[rank]
    to_row(lambda peer: res.at[peer], land.at[unit, way], ss, sr)
    wait_row(sr)

    for k, lo, hi in spans:
        wide[0, :, lo : lo + LANES] = land[:, 0, k, :]
        wide[1, :, lo : lo + LANES] = land[:, 1, k, :]
    state_in = parts(wide[0, :, 0:channels], 2)
    grad_in = parts(wide[1, :, 0:channels], 2)
    bc_buf[tp, 0] = b_own + mm(grad_in, scaled_out, NT)
    bc_buf[tp, 1] = c_own + mm(state_in, grads_in, NT)
    bc_copies = []
    for k in range(1, ways):
        copy = pltpu.make_async_remote_copy(
            src_ref=bc_buf.at[tp],
            dst_ref=bc_buf.at[tp],
            send_sem=bs.at[k - 1],
            recv_sem=br.at[k - 1],
            device_id=(me, way_peer(k)),
            device_id_type=MESH,
        )
        copy.start()
        bc_copies.append(copy)
    ssm = (ssm_own + carry_in * mm((c_rows,), state_in, TN)).astype(BF16).astype(F32)
    x_part = x_own + carry_out * mm((b_rows,), grad_in, TN)
    x_grad = (x_part * scales + skip * y_grads).astype(BF16).astype(F32)
    pre_grad = (x_grad * pre_slope).astype(BF16)
    gate_grad = (ssm * gate_slope).astype(BF16)
    sums = []
    for i, (lo, hi) in enumerate(CHUNKS):
        part = dot(pre_grad, wi[:, lo:hi], NN) + dot(gate_grad, wg[:, lo:hi], NN)
        rs_send[:, :, lo:hi] = part.reshape(ways, block, hi - lo).astype(BF16)
        for k in range(1, ways):
            copy = pltpu.make_async_remote_copy(
                src_ref=rs_send.at[way_peer(k), :, lo:hi],
                dst_ref=rs_recv.at[k - 1, :, lo:hi],
                send_sem=rs.at[i, k - 1],
                recv_sem=rr.at[i, k - 1],
                device_id=(me, way_peer(k)),
                device_id_type=MESH,
            )
            copy.start()
            sums.append(copy)
    for copy in bc_copies:
        copy.wait_recv()
    both = bc_buf[0]
    for k in range(1, ways):
        both = both + bc_buf[k]
    bg_ref[...] = both[0]
    cg_ref[...] = both[1]
    for i, (lo, hi) in enumerate(CHUNKS):
        for copy in sums[i * (ways - 1) : (i + 1) * (ways - 1)]:
            copy.wait_recv()
        value = rs_send[tp, :, lo:hi].astype(F32)
        for k in range(ways - 1):
            value = value + rs_recv[k, :, lo:hi].astype(F32)
        out_ref[:, lo:hi] = value.astype(BF16)

    for copy in gathers + decay_copies + total_copies + bc_copies + sums:
        copy.wait_send()
    for sem in (fs, ps, ss):
        wait_row(sem)


def shards(
    layer_input,
    out_grad,
    w_in,
    w_gate,
    w_out,
    b_proj,
    c_proj,
    log_decay,
    d_skip,
    entry_state,
    doc_start,
):
    block, width = layer_input.shape
    channels = w_in.shape[0]
    state, tokens = b_proj.shape
    ways = lax.axis_size("tp")
    row_len = 2 * state
    groups = lax.axis_size("seq") // row_len
    tiles = -(-channels // LANES)
    anywhere = pl.BlockSpec(memory_space=pl.ANY)
    inside = pl.BlockSpec(memory_space=pltpu.VMEM)
    dma = pltpu.SemaphoreType.DMA
    return pl.pallas_call(
        functools.partial(kernel, row_len, groups, ways),
        out_shape=(
            jax.ShapeDtypeStruct((block, width), BF16),
            jax.ShapeDtypeStruct((state, tokens), F32),
            jax.ShapeDtypeStruct((state, tokens), F32),
        ),
        in_specs=[anywhere] * 5 + [inside] * 6,
        out_specs=(inside, inside, inside),
        scratch_shapes=[
            pltpu.VMEM((ways, block, width), BF16),
            pltpu.VMEM((ways, block, width), BF16),
            pltpu.VMEM((channels, width), BF16),
            pltpu.VMEM((channels, width), BF16),
            pltpu.VMEM((channels, width), BF16),
            pltpu.VMEM((state, tiles, LANES), F32),
            pltpu.VMEM((tiles, LANES), F32),
            pltpu.VMEM((row_len, tiles, LANES), F32),
            pltpu.VMEM((row_len, tiles, LANES), F32),
            pltpu.VMEM((groups, tiles, LANES), F32),
            pltpu.VMEM((state, 2, tiles, LANES), F32),
            pltpu.VMEM((row_len, tiles, LANES), F32),
            pltpu.VMEM((row_len, tiles, LANES), F32),
            pltpu.VMEM((state, 2, tiles, LANES), F32),
            pltpu.VMEM((groups, tiles, LANES), F32),
            pltpu.VMEM((2, state, tiles * LANES), F32),
            pltpu.VMEM((ways, 2, state, tokens), F32),
            pltpu.VMEM((ways, block, width), BF16),
            pltpu.VMEM((ways - 1, block, width), BF16),
            dma((5,)),
            dma((2, ways - 1)),
            dma((2, ways - 1)),
            dma,
            dma,
            dma((groups - 1,)),
            dma((groups - 1,)),
            dma,
            dma,
            dma((groups - 1,)),
            dma((groups - 1,)),
            dma,
            dma,
            dma((ways - 1,)),
            dma((ways - 1,)),
            dma((len(CHUNKS), ways - 1)),
            dma((len(CHUNKS), ways - 1)),
        ],
        compiler_params=pltpu.CompilerParams(
            collective_id=0, has_side_effects=True, vmem_limit_bytes=32 * 1024 * 1024
        ),
        name="gated_recurrence_backward",
    )(
        layer_input,
        out_grad,
        w_in,
        w_gate,
        w_out,
        b_proj,
        c_proj,
        log_decay,
        d_skip.reshape(1, channels),
        entry_state,
        doc_start.reshape(1, tokens),
    )


def solution(mesh):
    in_specs = (
        P(("seq", "tp"), None),
        P(("seq", "tp"), None),
        P("tp", None),
        P("tp", None),
        P("tp", None),
        P(None, "seq"),
        P(None, "seq"),
        P(None, "seq"),
        P("tp"),
        P(None, "tp"),
        P("seq"),
    )
    out_specs = (P(("seq", "tp"), None), P(None, "seq"), P(None, "seq"))
    return jax.shard_map(shards, mesh=mesh, in_specs=in_specs, out_specs=out_specs, check_vma=False)
```

```python
import functools

import jax
import jax.numpy as jnp
from jax import lax
from jax.experimental import pallas as pl
from jax.experimental.pallas import tpu as pltpu
from jax.sharding import PartitionSpec as P

HDIM = 64
LANES = 128
SETS_Z = 4
MESH = pl.DeviceIdType.MESH
F32 = jnp.float32
BF16 = jnp.bfloat16
NN = (((1,), (0,)), ((), ()))
NT = (((1,), (1,)), ((), ()))
TN = (((0,), (0,)), ((), ()))
CHUNKS = ((0, 768), (768, 1600))


def dot(a, b, dims):
    return lax.dot_general(a, b, dims, preferred_element_type=F32)


def parts(value, count):
    high = value.astype(BF16)
    if count == 1:
        return (high,)
    return (high, (value - high.astype(F32)).astype(BF16))


def mm(a, b, dims):
    total = None
    for i, left in enumerate(a):
        for j, right in enumerate(b):
            if i + j < 2:
                term = dot(left, right, dims)
                total = term if total is None else total + term
    return total


def one_minus_exp(u):
    series = 1.0 - u / 6.0
    for k in (5.0, 4.0, 3.0, 2.0):
        series = 1.0 - u / k * series
    return jnp.where(u < 0.25, u * series, 1.0 - jnp.exp(-u))


def kernel(
    row_len,
    groups,
    sets_z,
    ways,
    x_hbm,
    g_hbm,
    wi_hbm,
    wg_hbm,
    wo_hbm,
    b_hbm,
    c_hbm,
    log_hbm,
    skip_hbm,
    entry_hbm,
    doc_hbm,
    out_hbm,
    bg_hbm,
    cg_hbm,
    xbuf,
    gbuf,
    wi,
    wg,
    wo,
    b_ref,
    c_ref,
    log_ref,
    skip_ref,
    entry_ref,
    doc_ref,
    entry_t,
    f_send,
    f_recv,
    f_pre,
    fy_buf,
    p_send,
    p_recv,
    res,
    land,
    t_buf,
    wide,
    bc_buf,
    rs_send,
    rs_recv,
    out_ref,
    bg_ref,
    cg_ref,
    osem,
    heard,
    lsem,
    gs,
    gr,
    fs,
    fr,
    ys,
    yr,
    ps,
    pr,
    ts,
    tr,
    ss,
    sr,
    bs,
    br,
    rs,
    rr,
):
    me = lax.axis_index("seq")
    tp = lax.axis_index("tp")
    group = lax.div(me, row_len)
    rank = lax.rem(me, row_len)
    way = lax.rem(rank, 2)
    share = 2 * b_hbm.shape[0] // row_len
    block = x_hbm.shape[0]
    tokens = ways * block
    channels = wi_hbm.shape[0]
    heads = log_ref.shape[0]
    state = b_ref.shape[0]
    tiles = p_recv.shape[1] // share
    spans = [(k, k * LANES, min(channels, (k + 1) * LANES)) for k in range(tiles)]

    small = [
        pltpu.make_async_copy(src, dst, lsem.at[5 + i])
        for i, (src, dst) in enumerate(
            (
                (log_hbm, log_ref),
                (doc_hbm, doc_ref),
                (b_hbm, b_ref),
                (c_hbm, c_ref),
                (skip_hbm, skip_ref),
                (entry_hbm, entry_ref),
            )
        )
    ]
    local = [
        pltpu.make_async_copy(x_hbm, xbuf.at[tp], lsem.at[3]),
        pltpu.make_async_copy(g_hbm, gbuf.at[tp], lsem.at[4]),
        pltpu.make_async_copy(wi_hbm, wi, lsem.at[0]),
        pltpu.make_async_copy(wg_hbm, wg, lsem.at[1]),
        pltpu.make_async_copy(wo_hbm, wo, lsem.at[2]),
    ]
    for copy in local[:2] + small + local[2:]:
        copy.start()

    def row_peer(i):
        return group * row_len + lax.rem(rank + i, row_len)

    def way_peer(k):
        return lax.rem(tp + k, ways)

    line, spot = lax.div(group, sets_z), lax.rem(group, sets_z)
    lines = groups // sets_z
    last_line, last_spot = lines - 1 - line, sets_z - 1 - spot

    def by_way(forward_value, backward_value):
        return forward_value * (1 - way) + backward_value * way

    def each_set(act):
        def step(i, carry):
            other_spot, other_line = lax.div(i, lines), lax.rem(i, lines)
            other = other_line * sets_z + other_spot
            gap = (other - group) * (1 - 2 * way)
            act(other, gap, other_spot)
            return carry

        lax.fori_loop(0, groups, step, 0)

    def device_of(other):
        return (other * row_len + rank, tp)

    barrier = pltpu.get_barrier_semaphore()

    def greet(i, carry):
        pl.semaphore_signal(barrier, inc=1, device_id=(row_peer(i), tp), device_id_type=MESH)
        return carry

    def greet_set(other, gap, other_spot):
        @pl.when(((gap < 0) & (spot <= other_spot)) | ((gap > 0) & (spot < other_spot)))
        def _():
            pl.semaphore_signal(barrier, inc=1, device_id=device_of(other), device_id_type=MESH)

    def answer_set(other, gap, other_spot):
        @pl.when((gap < 0) & (spot > other_spot))
        def _():
            pl.semaphore_signal(heard, inc=1, device_id=device_of(other), device_id_type=MESH)

    for k in range(1, ways):
        pl.semaphore_signal(barrier, inc=1, device_id=(me, way_peer(k)), device_id_type=MESH)
    lax.fori_loop(1, row_len, greet, 0)
    each_set(greet_set)
    before = by_way(
        last_line * (spot + 1) + (line + 1) * spot,
        line * (spot + 1) + spot + last_line * spot,
    )
    after = by_way((last_line + 1) * last_spot, line * last_spot)
    pl.semaphore_wait(barrier, row_len + ways - 2 + before)

    half = block // 2
    right, left = way_peer(1), way_peer(ways - 1)
    gathers = []

    def pass_on(array, slot, part, to, landing):
        buf = (xbuf, gbuf)[array]
        where = buf.at[slot, pl.ds(part * half, half)]
        copy = pltpu.make_async_remote_copy(
            src_ref=where,
            dst_ref=where,
            send_sem=gs.at[array, landing],
            recv_sem=gr.at[array, landing],
            device_id=(me, to),
            device_id_type=MESH,
        )
        copy.start()
        gathers.append(copy)

    def landed(array, slot, part, landing):
        where = (xbuf, gbuf)[array].at[slot, pl.ds(part * half, half)]
        pltpu.make_async_copy(where, where, gr.at[array, landing]).wait()

    def forward(array):
        landed(array, left, 0, 0)
        pass_on(array, left, 0, right, 4)
        landed(array, right, 1, 3)
        pass_on(array, right, 1, left, 5)

    def gathered(array):
        landed(array, left, 1, 1)
        landed(array, right, 0, 2)
        landed(array, way_peer(2), 0, 4)
        landed(array, way_peer(2), 1, 5)

    for array in range(2):
        local[array].wait()
        pass_on(array, tp, 0, right, 0)
        pass_on(array, tp, 1, left, 3)
        pass_on(array, tp, 1, right, 1)
        pass_on(array, tp, 0, left, 2)
    each_set(answer_set)

    def to_row(src_at, dst, send_sem, recv_sem):
        def send(i, carry):
            pltpu.make_async_remote_copy(
                src_ref=src_at(lax.rem(rank + i, row_len)),
                dst_ref=dst,
                send_sem=send_sem,
                recv_sem=recv_sem,
                device_id=(row_peer(i), tp),
                device_id_type=MESH,
            ).start()
            return carry

        lax.fori_loop(1, row_len, send, 0)

    def set_copy(buf, other, source, send_sem, recv_sem):
        return pltpu.make_async_remote_copy(
            src_ref=buf.at[source],
            dst_ref=buf.at[source],
            send_sem=send_sem.at[other],
            recv_sem=recv_sem.at[source],
            device_id=device_of(other),
            device_id_type=MESH,
        )

    def to_sets(buf, send_sem, recv_sem):
        def send(other, gap, other_spot):
            @pl.when(gap > 0)
            def _():
                set_copy(buf, other, group, send_sem, recv_sem).start()

        each_set(send)

    def wait_sets(buf, send_sem, recv_sem, sent):
        def wait(other, gap, other_spot):
            if sent:

                @pl.when(gap > 0)
                def _():
                    set_copy(buf, other, group, send_sem, recv_sem).wait_send()

            else:

                @pl.when(gap < 0)
                def _():
                    set_copy(buf, other, other, send_sem, recv_sem).wait_recv()

        each_set(wait)

    def wait_row(sem):
        every = p_recv.at[pl.ds(0, row_len - 1)]
        pltpu.make_async_copy(every, every, sem).wait()

    for copy in small:
        copy.wait()
    head_row = lax.broadcasted_iota(jnp.int32, (heads, channels), 0)
    chan_row = lax.broadcasted_iota(jnp.int32, (heads, channels), 1) + tp * channels
    low = head_row * HDIM
    pick = jnp.where((chan_row >= low) & (chan_row < low + HDIM), 1.0, 0.0).astype(BF16)
    logs = dot(log_ref[...], pick, TN)
    row_at = lax.broadcasted_iota(jnp.int32, (tokens, tokens), 0)
    col_at = lax.broadcasted_iota(jnp.int32, (tokens, tokens), 1)
    tri = jnp.where(row_at >= col_at, 1.0, 0.0).astype(BF16)
    eye = jnp.where(row_at == col_at, 1.0, 0.0).astype(BF16)
    cumulative = dot(tri, logs.astype(BF16), NN)
    at = lax.broadcasted_iota(jnp.int32, (1, tokens), 1) + me
    marks = jnp.where(at > 0, doc_ref[...], 0).astype(F32)
    marks_wide = jnp.broadcast_to(marks, (channels, tokens)).astype(BF16)
    marks_sq = jnp.broadcast_to(marks, (tokens, tokens)).astype(BF16)
    counts = dot(tri, marks_wide, NT)
    mark_col = dot(eye, marks_wide, NT)
    counts_col = dot(tri, marks_sq, NT)
    counts_row = dot(marks_sq, tri, NT)
    last = counts[tokens - 1 : tokens, :]
    total = cumulative[tokens - 1 : tokens, :]
    factor = jnp.where(last == 0.0, jnp.exp(total), 0.0)

    f_send[...] = jnp.zeros_like(f_send)
    for k, lo, hi in spans:
        f_send[share * k : share * (k + 1), 0 : hi - lo] = jnp.broadcast_to(
            factor[:, lo:hi], (share, hi - lo)
        )
    f_recv[rank] = f_send[...]
    to_row(lambda peer: f_send, f_recv.at[rank], fs, fr)
    forward(0)

    p_send[...] = jnp.zeros_like(p_send)
    entry_t[...] = jnp.zeros_like(entry_t)

    def lay_out(rows, put):
        for q in range(state // share):
            for k, lo, hi in spans:
                put(q, slice(share * k, share * (k + 1)), slice(0, hi - lo), rows[share * q : share * (q + 1), lo:hi])

    def put_entry(q, rows, lanes, value):
        entry_t[q, rows, lanes] = value

    def put_state(q, rows, lanes, value):
        p_send[2 * q, rows, lanes] = value

    def put_grad(q, rows, lanes, value):
        p_send[2 * q + 1, rows, lanes] = value

    lay_out(entry_ref[...], put_entry)

    scales = jnp.where(mark_col == 1.0, 1.0, jnp.sqrt(one_minus_exp(-2.0 * logs)))
    centre = cumulative[tokens // 2 : tokens // 2 + 1, :]
    rising = jnp.exp(cumulative - centre)
    falling = jnp.exp(centre - cumulative)
    carry_in = jnp.where(counts == 0.0, jnp.exp(cumulative), 0.0)
    carry_out = jnp.where(counts == last, jnp.exp(total - cumulative), 0.0)
    causal = (row_at >= col_at) & (counts_col == counts_row)
    b_rows = b_ref[...]
    c_rows = c_ref[...]
    crossed = jnp.where(causal, dot(c_rows, b_rows, TN), 0.0)
    skip = skip_ref[...]

    forward(1)

    wait_row(fr)

    def at_step(i, count):
        return jnp.where(way == 0, i, count - 1 - i)

    def decay_step(i, product):
        j = at_step(i, row_len)
        f_pre[j] = product
        return product * f_recv[j]

    fy_buf[group] = lax.fori_loop(0, row_len, decay_step, jnp.ones(f_send.shape, F32))

    @pl.when(after > 0)
    def _():
        pl.semaphore_wait(heard, after)

    to_sets(fy_buf, ys, yr)

    gathered(0)
    local[2].wait()
    rows = xbuf[...].reshape(tokens, x_hbm.shape[1])
    pre_act = dot(rows, wi[...], NT)
    local[3].wait()
    gate_act = dot(rows, wg[...], NT)
    pre_sig = jax.nn.sigmoid(pre_act)
    gate_sig = jax.nn.sigmoid(gate_act)
    x_rows = (pre_act * pre_sig).astype(BF16).astype(F32)
    gate_silu = gate_act * gate_sig
    scaled = x_rows * scales
    scaled_out = parts(scaled * carry_out, 2)
    state_part = mm((b_rows,), scaled_out, NN)
    lay_out(state_part, put_state)
    gathered(1)
    local[4].wait()
    mix_grad = dot(gbuf[...].reshape(tokens, g_hbm.shape[1]), wo[...], NT)
    y_grads = (mix_grad * gate_silu).astype(BF16).astype(F32)
    grads_in = parts(y_grads * carry_in, 2)
    grad_part = mm((c_rows,), grads_in, NN)
    lay_out(grad_part, put_grad)

    p_recv[rank] = p_send[rank]
    to_row(lambda peer: p_send.at[peer], p_recv.at[rank], ps, pr)

    upper = parts(y_grads * rising, 2)
    lower = parts(scaled * falling, 2)
    weight = parts(jnp.where(causal, mm(upper, lower, NT), 0.0), 2)
    crossed_parts = parts(crossed, 2)
    ssm_own = rising * mm(crossed_parts, lower, NN) + skip * x_rows
    x_own = falling * mm(crossed_parts, upper, TN)
    c_own = mm((b_rows,), weight, NT)
    b_own = mm((c_rows,), weight, NN)
    pre_slope = pre_sig * (1.0 + pre_act * (1.0 - pre_sig))
    gate_slope = mix_grad * (gate_sig * (1.0 + gate_act * (1.0 - gate_sig)))

    wait_row(pr)

    def scan_step(i, carried):
        j = at_step(i, row_len)
        res[j] = carried
        return f_recv[j] * carried + p_recv[j]

    t_buf[group] = lax.fori_loop(0, row_len, scan_step, jnp.zeros(f_send.shape, F32))
    to_sets(t_buf, ts, tr)
    wait_sets(fy_buf, ys, yr, False)
    wait_sets(t_buf, ts, tr, False)
    carried = jnp.where(way == 0, entry_t[lax.div(rank, 2)], 0.0)
    ahead = at_step(group, groups)
    for i in range(groups):
        j = at_step(i, groups)
        carried = jnp.where(i < ahead, fy_buf[j] * carried + t_buf[j], carried)
    res[...] = res[...] + f_pre[...] * carried[None]
    land[rank] = res[rank]
    to_row(lambda peer: res.at[peer], land.at[rank], ss, sr)
    wait_row(sr)

    for q in range(state // share):
        for k, lo, hi in spans:
            for side in range(2):
                wide[side, share * q : share * (q + 1), lo : lo + LANES] = land[
                    2 * q + side, share * k : share * (k + 1), :
                ]
    state_in = parts(wide[0, :, 0:channels], 2)
    grad_in = parts(wide[1, :, 0:channels], 2)
    ssm = (ssm_own + carry_in * mm((c_rows,), state_in, TN)).astype(BF16).astype(F32)
    x_part = x_own + carry_out * mm((b_rows,), grad_in, TN)
    x_grad = (x_part * scales + skip * y_grads).astype(BF16).astype(F32)
    pre_grad = (x_grad * pre_slope).astype(BF16)
    gate_grad = (ssm * gate_slope).astype(BF16)
    bc_buf[tp, 0] = b_own + mm(grad_in, scaled_out, NT)
    bc_buf[tp, 1] = c_own + mm(state_in, grads_in, NT)
    bc_copies = []
    for k in range(1, ways):
        copy = pltpu.make_async_remote_copy(
            src_ref=bc_buf.at[tp],
            dst_ref=bc_buf.at[tp],
            send_sem=bs.at[k - 1],
            recv_sem=br.at[k - 1],
            device_id=(me, way_peer(k)),
            device_id_type=MESH,
        )
        copy.start()
        bc_copies.append(copy)
    order = (
        jnp.where(tp == 0, 3, jnp.where(tp == ways - 1, 1, 2)),
        jnp.where((tp == 0) | (tp == ways - 1), 2, 1),
        jnp.where(tp == 0, 1, 3),
    )
    sums = []
    for i, (lo, hi) in enumerate(CHUNKS):
        part = dot(pre_grad, wi[:, lo:hi], NN) + dot(gate_grad, wg[:, lo:hi], NN)
        rs_send[:, :, lo:hi] = part.reshape(ways, block, hi - lo).astype(BF16)
        for k in order:
            copy = pltpu.make_async_remote_copy(
                src_ref=rs_send.at[way_peer(k), :, lo:hi],
                dst_ref=rs_recv.at[k - 1, :, lo:hi],
                send_sem=rs.at[i, k - 1],
                recv_sem=rr.at[i, k - 1],
                device_id=(me, way_peer(k)),
                device_id_type=MESH,
            )
            copy.start()
            sums.append(copy)
    for copy in bc_copies:
        copy.wait_recv()
    both = bc_buf[0]
    for k in range(1, ways):
        both = both + bc_buf[k]
    bg_ref[...] = both[0]
    cg_ref[...] = both[1]
    outs = [
        pltpu.make_async_copy(bg_ref, bg_hbm, osem.at[0]),
        pltpu.make_async_copy(cg_ref, cg_hbm, osem.at[1]),
    ]
    for copy in outs:
        copy.start()
    for i, (lo, hi) in enumerate(CHUNKS):
        for copy in sums[i * (ways - 1) : (i + 1) * (ways - 1)]:
            copy.wait_recv()
        value = rs_send[tp, :, lo:hi].astype(F32)
        for k in range(ways - 1):
            value = value + rs_recv[k, :, lo:hi].astype(F32)
        out_ref[:, lo:hi] = value.astype(BF16)
    outs.append(pltpu.make_async_copy(out_ref, out_hbm, osem.at[2]))
    outs[2].start()

    for copy in gathers + bc_copies + sums:
        copy.wait_send()
    wait_sets(fy_buf, ys, yr, True)
    wait_sets(t_buf, ts, tr, True)
    for sem in (fs, ps, ss):
        wait_row(sem)
    for copy in outs:
        copy.wait()


def keep(*refs):
    count = len(refs) // 3
    results, outs, held = refs[:count], refs[count : 2 * count], refs[2 * count : 3 * count]
    sems = refs[-1]
    loads = [
        pltpu.make_async_copy(src, dst, sems.at[i]) for i, (src, dst) in enumerate(zip(results, held))
    ]
    stores = [
        pltpu.make_async_copy(src, dst, sems.at[count + i])
        for i, (src, dst) in enumerate(zip(held, outs))
    ]
    for copy in loads:
        copy.start()
    for load, store in zip(loads, stores):
        load.wait()
        store.start()
    for copy in stores:
        copy.wait()


def shards(
    layer_input,
    out_grad,
    w_in,
    w_gate,
    w_out,
    b_proj,
    c_proj,
    log_decay,
    d_skip,
    entry_state,
    doc_start,
):
    block, width = layer_input.shape
    channels = w_in.shape[0]
    state, tokens = b_proj.shape
    ways = lax.axis_size("tp")
    row_len = 8
    share = 2 * state // row_len
    groups = lax.axis_size("seq") // row_len
    tiles = -(-channels // LANES)
    anywhere = pl.BlockSpec(memory_space=pltpu.HBM)
    dma = pltpu.SemaphoreType.DMA
    results = pl.pallas_call(
        functools.partial(kernel, row_len, groups, SETS_Z, ways),
        out_shape=(
            jax.ShapeDtypeStruct((block, width), BF16),
            jax.ShapeDtypeStruct((state, tokens), F32),
            jax.ShapeDtypeStruct((state, tokens), F32),
        ),
        in_specs=[anywhere] * 11,
        out_specs=(anywhere, anywhere, anywhere),
        scratch_shapes=[
            pltpu.VMEM((ways, block, width), BF16),
            pltpu.VMEM((ways, block, width), BF16),
            pltpu.VMEM((channels, width), BF16),
            pltpu.VMEM((channels, width), BF16),
            pltpu.VMEM((channels, width), BF16),
            pltpu.VMEM(b_proj.shape, BF16),
            pltpu.VMEM(c_proj.shape, BF16),
            pltpu.VMEM(log_decay.shape, BF16),
            pltpu.VMEM((1, channels), F32),
            pltpu.VMEM(entry_state.shape, F32),
            pltpu.VMEM((1, tokens), jnp.int32),
            pltpu.VMEM((state // share, tiles * share, LANES), F32),
            pltpu.VMEM((tiles * share, LANES), F32),
            pltpu.VMEM((row_len, tiles * share, LANES), F32),
            pltpu.VMEM((row_len, tiles * share, LANES), F32),
            pltpu.VMEM((groups, tiles * share, LANES), F32),
            pltpu.VMEM((row_len, tiles * share, LANES), F32),
            pltpu.VMEM((row_len, tiles * share, LANES), F32),
            pltpu.VMEM((row_len, tiles * share, LANES), F32),
            pltpu.VMEM((row_len, tiles * share, LANES), F32),
            pltpu.VMEM((groups, tiles * share, LANES), F32),
            pltpu.VMEM((2, state, tiles * LANES), F32),
            pltpu.VMEM((ways, 2, state, tokens), F32),
            pltpu.VMEM((ways, block, width), BF16),
            pltpu.VMEM((ways - 1, block, width), BF16),
            pltpu.VMEM((block, width), BF16),
            pltpu.VMEM((state, tokens), F32),
            pltpu.VMEM((state, tokens), F32),
            dma((3,)),
            pltpu.SemaphoreType.REGULAR,
            dma((11,)),
            dma((2, 6)),
            dma((2, 6)),
            dma,
            dma,
            dma((groups,)),
            dma((groups,)),
            dma,
            dma,
            dma((groups,)),
            dma((groups,)),
            dma,
            dma,
            dma((ways - 1,)),
            dma((ways - 1,)),
            dma((len(CHUNKS), ways - 1)),
            dma((len(CHUNKS), ways - 1)),
        ],
        compiler_params=pltpu.CompilerParams(
            collective_id=0, has_side_effects=True, vmem_limit_bytes=64 * 1024 * 1024
        ),
        name="gated_recurrence_backward",
    )(
        layer_input,
        out_grad,
        w_in,
        w_gate,
        w_out,
        b_proj,
        c_proj,
        log_decay,
        d_skip.reshape(1, channels),
        entry_state,
        doc_start.reshape(1, tokens),
    )
    return pl.pallas_call(
        keep,
        out_shape=tuple(jax.ShapeDtypeStruct(r.shape, r.dtype) for r in results),
        in_specs=[anywhere] * 3,
        out_specs=(anywhere,) * 3,
        scratch_shapes=[pltpu.VMEM(r.shape, r.dtype) for r in results] + [dma((6,))],
        compiler_params=pltpu.CompilerParams(vmem_limit_bytes=64 * 1024 * 1024),
        name="results",
    )(*results)


def solution(mesh):
    in_specs = (
        P(("seq", "tp"), None),
        P(("seq", "tp"), None),
        P("tp", None),
        P("tp", None),
        P("tp", None),
        P(None, "seq"),
        P(None, "seq"),
        P(None, "seq"),
        P("tp"),
        P(None, "tp"),
        P("seq"),
    )
    out_specs = (P(("seq", "tp"), None), P(None, "seq"), P(None, "seq"))
    return jax.shard_map(shards, mesh=mesh, in_specs=in_specs, out_specs=out_specs, check_vma=False)
```

```python
import functools

import jax
import jax.numpy as jnp
from jax import lax
from jax.experimental import pallas as pl
from jax.experimental.pallas import tpu as pltpu
from jax.sharding import PartitionSpec as P

HDIM = 64
LANES = 128
SETS_Z = 4
MESH = pl.DeviceIdType.MESH
F32 = jnp.float32
BF16 = jnp.bfloat16
NN = (((1,), (0,)), ((), ()))
NT = (((1,), (1,)), ((), ()))
TN = (((0,), (0,)), ((), ()))
CHUNKS = ((0, 768), (768, 1600))


def dot(a, b, dims):
    return lax.dot_general(a, b, dims, preferred_element_type=F32)


def parts(value, count):
    high = value.astype(BF16)
    if count == 1:
        return (high,)
    return (high, (value - high.astype(F32)).astype(BF16))


def mm(a, b, dims):
    total = None
    for i, left in enumerate(a):
        for j, right in enumerate(b):
            if i + j < 2:
                term = dot(left, right, dims)
                total = term if total is None else total + term
    return total


def one_minus_exp(u):
    series = 1.0 - u / 6.0
    for k in (5.0, 4.0, 3.0, 2.0):
        series = 1.0 - u / k * series
    return jnp.where(u < 0.25, u * series, 1.0 - jnp.exp(-u))


def kernel(
    row_len,
    groups,
    sets_z,
    ways,
    x_hbm,
    g_hbm,
    wi_hbm,
    wg_hbm,
    wo_hbm,
    b_hbm,
    c_hbm,
    log_hbm,
    skip_hbm,
    entry_hbm,
    doc_hbm,
    out_ref,
    bg_ref,
    cg_ref,
    xbuf,
    gbuf,
    wi,
    wg,
    wo,
    b_ref,
    c_ref,
    log_ref,
    skip_ref,
    entry_ref,
    doc_ref,
    entry_t,
    f_send,
    f_recv,
    f_pre,
    fy_buf,
    p_send,
    p_recv,
    res,
    land,
    t_buf,
    wide,
    bc_buf,
    from_gate,
    rs_send,
    rs_recv,
    heard,
    lsem,
    gs,
    gr,
    fs,
    fr,
    ys,
    yr,
    ps,
    pr,
    ts,
    tr,
    ss,
    sr,
    bs,
    br,
    rs,
    rr,
):
    me = lax.axis_index("seq")
    tp = lax.axis_index("tp")
    group = lax.div(me, row_len)
    rank = lax.rem(me, row_len)
    way = lax.rem(rank, 2)
    share = 2 * b_hbm.shape[0] // row_len
    block = x_hbm.shape[0]
    tokens = ways * block
    channels = wi_hbm.shape[0]
    heads = log_ref.shape[0]
    state = b_ref.shape[0]
    tiles = p_recv.shape[1] // share
    spans = [(k, k * LANES, min(channels, (k + 1) * LANES)) for k in range(tiles)]

    small = [
        pltpu.make_async_copy(src, dst, lsem.at[5 + i])
        for i, (src, dst) in enumerate(
            (
                (log_hbm, log_ref),
                (doc_hbm, doc_ref),
                (b_hbm, b_ref),
                (c_hbm, c_ref),
                (skip_hbm, skip_ref),
                (entry_hbm, entry_ref),
            )
        )
    ]
    local = [
        pltpu.make_async_copy(x_hbm, xbuf.at[tp], lsem.at[3]),
        pltpu.make_async_copy(g_hbm, gbuf.at[tp], lsem.at[4]),
        pltpu.make_async_copy(wi_hbm, wi, lsem.at[0]),
        pltpu.make_async_copy(wg_hbm, wg, lsem.at[1]),
        pltpu.make_async_copy(wo_hbm, wo, lsem.at[2]),
    ]
    for copy in local[:2] + small + local[2:]:
        copy.start()

    def row_peer(i):
        return group * row_len + lax.rem(rank + i, row_len)

    def way_peer(k):
        return lax.rem(tp + k, ways)

    line, spot = lax.div(group, sets_z), lax.rem(group, sets_z)
    lines = groups // sets_z
    last_line, last_spot = lines - 1 - line, sets_z - 1 - spot

    def by_way(forward_value, backward_value):
        return forward_value * (1 - way) + backward_value * way

    def each_set(act):
        def step(i, carry):
            other_spot, other_line = lax.div(i, lines), lax.rem(i, lines)
            other = other_line * sets_z + other_spot
            gap = (other - group) * (1 - 2 * way)
            act(other, gap, other_spot)
            return carry

        lax.fori_loop(0, groups, step, 0)

    def device_of(other):
        return (other * row_len + rank, tp)

    barrier = pltpu.get_barrier_semaphore()

    def greet(i, carry):
        pl.semaphore_signal(barrier, inc=1, device_id=(row_peer(i), tp), device_id_type=MESH)
        return carry

    def greet_set(other, gap, other_spot):
        @pl.when(((gap < 0) & (spot <= other_spot)) | ((gap > 0) & (spot < other_spot)))
        def _():
            pl.semaphore_signal(barrier, inc=1, device_id=device_of(other), device_id_type=MESH)

    def answer_set(other, gap, other_spot):
        @pl.when((gap < 0) & (spot > other_spot))
        def _():
            pl.semaphore_signal(heard, inc=1, device_id=device_of(other), device_id_type=MESH)

    for k in range(1, ways):
        pl.semaphore_signal(barrier, inc=1, device_id=(me, way_peer(k)), device_id_type=MESH)
    lax.fori_loop(1, row_len, greet, 0)
    each_set(greet_set)
    before = by_way(
        last_line * (spot + 1) + (line + 1) * spot,
        line * (spot + 1) + spot + last_line * spot,
    )
    after = by_way((last_line + 1) * last_spot, line * last_spot)
    pl.semaphore_wait(barrier, row_len + ways - 2 + before)

    half = block // 2
    right, left = way_peer(1), way_peer(ways - 1)
    gathers = []

    def pass_on(array, slot, part, to, landing):
        buf = (xbuf, gbuf)[array]
        where = buf.at[slot, pl.ds(part * half, half)]
        copy = pltpu.make_async_remote_copy(
            src_ref=where,
            dst_ref=where,
            send_sem=gs.at[array, landing],
            recv_sem=gr.at[array, landing],
            device_id=(me, to),
            device_id_type=MESH,
        )
        copy.start()
        gathers.append(copy)

    def landed(array, slot, part, landing):
        where = (xbuf, gbuf)[array].at[slot, pl.ds(part * half, half)]
        pltpu.make_async_copy(where, where, gr.at[array, landing]).wait()

    def forward(array):
        landed(array, left, 0, 0)
        pass_on(array, left, 0, right, 4)
        landed(array, right, 1, 3)
        pass_on(array, right, 1, left, 5)

    def gathered(array):
        landed(array, left, 1, 1)
        landed(array, right, 0, 2)
        landed(array, way_peer(2), 0, 4)
        landed(array, way_peer(2), 1, 5)

    for array in range(2):
        local[array].wait()
        pass_on(array, tp, 0, right, 0)
        pass_on(array, tp, 1, left, 3)
        pass_on(array, tp, 1, right, 1)
        pass_on(array, tp, 0, left, 2)
    each_set(answer_set)

    def to_row(src_at, dst, send_sem, recv_sem):
        def send(i, carry):
            pltpu.make_async_remote_copy(
                src_ref=src_at(lax.rem(rank + i, row_len)),
                dst_ref=dst,
                send_sem=send_sem,
                recv_sem=recv_sem,
                device_id=(row_peer(i), tp),
                device_id_type=MESH,
            ).start()
            return carry

        lax.fori_loop(1, row_len, send, 0)

    def to_owners(side, src_at, dst, send_sem, recv_sem):
        def send(i, carry):
            peer = 2 * lax.rem(lax.div(rank, 2) + i, row_len // 2) + side

            @pl.when(peer != rank)
            def _():
                pltpu.make_async_remote_copy(
                    src_ref=src_at(peer),
                    dst_ref=dst,
                    send_sem=send_sem,
                    recv_sem=recv_sem,
                    device_id=(group * row_len + peer, tp),
                    device_id_type=MESH,
                ).start()

            return carry

        lax.fori_loop(0, row_len // 2, send, 0)

    def set_copy(buf, other, source, send_sem, recv_sem):
        return pltpu.make_async_remote_copy(
            src_ref=buf.at[source],
            dst_ref=buf.at[source],
            send_sem=send_sem.at[other],
            recv_sem=recv_sem.at[source],
            device_id=device_of(other),
            device_id_type=MESH,
        )

    def to_sets(buf, send_sem, recv_sem):
        def send(other, gap, other_spot):
            @pl.when(gap > 0)
            def _():
                set_copy(buf, other, group, send_sem, recv_sem).start()

        each_set(send)

    def wait_sets(buf, send_sem, recv_sem, sent):
        def wait(other, gap, other_spot):
            if sent:

                @pl.when(gap > 0)
                def _():
                    set_copy(buf, other, group, send_sem, recv_sem).wait_send()

            else:

                @pl.when(gap < 0)
                def _():
                    set_copy(buf, other, other, send_sem, recv_sem).wait_recv()

        each_set(wait)

    def wait_row(sem):
        every = p_recv.at[pl.ds(0, row_len - 1)]
        pltpu.make_async_copy(every, every, sem).wait()

    for copy in small:
        copy.wait()
    head_row = lax.broadcasted_iota(jnp.int32, (heads, channels), 0)
    chan_row = lax.broadcasted_iota(jnp.int32, (heads, channels), 1) + tp * channels
    low = head_row * HDIM
    pick = jnp.where((chan_row >= low) & (chan_row < low + HDIM), 1.0, 0.0).astype(BF16)
    logs = dot(log_ref[...], pick, TN)
    row_at = lax.broadcasted_iota(jnp.int32, (tokens, tokens), 0)
    col_at = lax.broadcasted_iota(jnp.int32, (tokens, tokens), 1)
    tri = jnp.where(row_at >= col_at, 1.0, 0.0).astype(BF16)
    eye = jnp.where(row_at == col_at, 1.0, 0.0).astype(BF16)
    cumulative = dot(tri, logs.astype(BF16), NN)
    at = lax.broadcasted_iota(jnp.int32, (1, tokens), 1) + me
    marks = jnp.where(at > 0, doc_ref[...], 0).astype(F32)
    marks_wide = jnp.broadcast_to(marks, (channels, tokens)).astype(BF16)
    marks_sq = jnp.broadcast_to(marks, (tokens, tokens)).astype(BF16)
    counts = dot(tri, marks_wide, NT)
    mark_col = dot(eye, marks_wide, NT)
    counts_col = dot(tri, marks_sq, NT)
    counts_row = dot(marks_sq, tri, NT)
    last = counts[tokens - 1 : tokens, :]
    total = cumulative[tokens - 1 : tokens, :]
    factor = jnp.where(last == 0.0, jnp.exp(total), 0.0)

    f_send[...] = jnp.zeros_like(f_send)
    for k, lo, hi in spans:
        f_send[share * k : share * (k + 1), 0 : hi - lo] = jnp.broadcast_to(
            factor[:, lo:hi], (share, hi - lo)
        )
    f_recv[rank] = f_send[...]
    to_row(lambda peer: f_send, f_recv.at[rank], fs, fr)
    forward(0)

    p_send[...] = jnp.zeros_like(p_send)
    entry_t[...] = jnp.zeros_like(entry_t)

    def lay_out(rows, put):
        for q in range(state // share):
            for k, lo, hi in spans:
                put(q, slice(share * k, share * (k + 1)), slice(0, hi - lo), rows[share * q : share * (q + 1), lo:hi])

    def put_entry(q, rows, lanes, value):
        entry_t[q, rows, lanes] = value

    def put_state(q, rows, lanes, value):
        p_send[2 * q, rows, lanes] = value

    def put_grad(q, rows, lanes, value):
        p_send[2 * q + 1, rows, lanes] = value

    lay_out(entry_ref[...], put_entry)

    scales = jnp.where(mark_col == 1.0, 1.0, jnp.sqrt(one_minus_exp(-2.0 * logs)))
    centre = cumulative[tokens // 2 : tokens // 2 + 1, :]
    rising = jnp.exp(cumulative - centre)
    falling = jnp.exp(centre - cumulative)
    carry_in = jnp.where(counts == 0.0, jnp.exp(cumulative), 0.0)
    carry_out = jnp.where(counts == last, jnp.exp(total - cumulative), 0.0)
    causal = (row_at >= col_at) & (counts_col == counts_row)
    b_rows = b_ref[...]
    c_rows = c_ref[...]
    crossed = jnp.where(causal, dot(c_rows, b_rows, TN), 0.0)
    skip = skip_ref[...]

    forward(1)

    wait_row(fr)

    def at_step(i, count):
        return jnp.where(way == 0, i, count - 1 - i)

    def decay_step(i, product):
        j = at_step(i, row_len)
        f_pre[j] = product
        return product * f_recv[j]

    fy_buf[group] = lax.fori_loop(0, row_len, decay_step, jnp.ones(f_send.shape, F32), unroll=True)

    @pl.when(after > 0)
    def _():
        pl.semaphore_wait(heard, after)

    to_sets(fy_buf, ys, yr)

    gathered(0)
    local[2].wait()
    rows = xbuf[...].reshape(tokens, x_hbm.shape[1])
    pre_act = dot(rows, wi[...], NT)
    local[3].wait()
    gate_act = dot(rows, wg[...], NT)
    pre_sig = jax.nn.sigmoid(pre_act)
    gate_sig = jax.nn.sigmoid(gate_act)
    x_rows = (pre_act * pre_sig).astype(BF16).astype(F32)
    gate_silu = gate_act * gate_sig
    scaled = x_rows * scales
    scaled_out = parts(scaled * carry_out, 2)
    state_part = mm((b_rows,), scaled_out, NN)
    lay_out(state_part, put_state)
    to_owners(0, lambda peer: p_send.at[peer], p_recv.at[rank], ps, pr)
    gathered(1)
    local[4].wait()
    mix_grad = dot(gbuf[...].reshape(tokens, g_hbm.shape[1]), wo[...], NT)
    y_grads = (mix_grad * gate_silu).astype(BF16).astype(F32)
    grads_in = parts(y_grads * carry_in, 2)
    grad_part = mm((c_rows,), grads_in, NN)
    lay_out(grad_part, put_grad)

    to_owners(1, lambda peer: p_send.at[peer], p_recv.at[rank], ps, pr)
    p_recv[rank] = p_send[rank]

    upper = parts(y_grads * rising, 2)
    lower = parts(scaled * falling, 2)
    weight = parts(jnp.where(causal, mm(upper, lower, NT), 0.0), 2)
    crossed_parts = parts(crossed, 2)
    ssm_own = rising * mm(crossed_parts, lower, NN) + skip * x_rows
    x_own = falling * mm(crossed_parts, upper, TN)
    c_own = mm((b_rows,), weight, NT)
    b_own = mm((c_rows,), weight, NN)
    pre_slope = pre_sig * (1.0 + pre_act * (1.0 - pre_sig))
    gate_slope = mix_grad * (gate_sig * (1.0 + gate_act * (1.0 - gate_sig)))

    wait_row(pr)

    def scan_step(i, carried):
        j = at_step(i, row_len)
        res[j] = carried
        return f_recv[j] * carried + p_recv[j]

    t_buf[group] = lax.fori_loop(0, row_len, scan_step, jnp.zeros(f_send.shape, F32), unroll=True)
    to_sets(t_buf, ts, tr)
    wait_sets(fy_buf, ys, yr, False)
    wait_sets(t_buf, ts, tr, False)
    carried = jnp.where(way == 0, entry_t[lax.div(rank, 2)], 0.0)
    ahead = at_step(group, groups)
    for i in range(groups):
        j = at_step(i, groups)
        carried = jnp.where(i < ahead, fy_buf[j] * carried + t_buf[j], carried)
    res[...] = res[...] + f_pre[...] * carried[None]
    land[rank] = res[rank]
    to_row(lambda peer: res.at[peer], land.at[rank], ss, sr.at[rank])

    def carried_in(side):
        for q in range(state // share):
            owner = 2 * q + side

            @pl.when(owner != rank)
            def _():
                pltpu.make_async_copy(land.at[owner], land.at[owner], sr.at[owner]).wait()

            for k, lo, hi in spans:
                wide[side, share * q : share * (q + 1), lo : lo + LANES] = land[
                    owner, share * k : share * (k + 1), :
                ]
        return parts(wide[side, :, 0:channels], 2)

    bc_copies = []

    def share_out(side, value):
        bc_buf[tp, side] = value
        for k in range(1, ways):
            copy = pltpu.make_async_remote_copy(
                src_ref=bc_buf.at[tp, side],
                dst_ref=bc_buf.at[tp, side],
                send_sem=bs.at[side, k - 1],
                recv_sem=br.at[side, k - 1],
                device_id=(me, way_peer(k)),
                device_id_type=MESH,
            )
            copy.start()
            bc_copies.append(copy)

    state_in = carried_in(0)
    share_out(1, c_own + mm(state_in, grads_in, NT))
    ssm = (ssm_own + carry_in * mm((c_rows,), state_in, TN)).astype(BF16).astype(F32)
    gate_grad = (ssm * gate_slope).astype(BF16)
    from_gate[...] = dot(gate_grad, wg[...], NN)
    grad_in = carried_in(1)
    x_part = x_own + carry_out * mm((b_rows,), grad_in, TN)
    x_grad = (x_part * scales + skip * y_grads).astype(BF16).astype(F32)
    pre_grad = (x_grad * pre_slope).astype(BF16)
    share_out(0, b_own + mm(grad_in, scaled_out, NT))
    order = (
        jnp.where(tp == 0, 3, jnp.where(tp == ways - 1, 1, 2)),
        jnp.where((tp == 0) | (tp == ways - 1), 2, 1),
        jnp.where(tp == 0, 1, 3),
    )
    sums = []
    for i, (lo, hi) in enumerate(CHUNKS):
        part = dot(pre_grad, wi[:, lo:hi], NN) + from_gate[:, lo:hi]
        rs_send[:, :, lo:hi] = part.reshape(ways, block, hi - lo).astype(BF16)
        for k in order:
            copy = pltpu.make_async_remote_copy(
                src_ref=rs_send.at[way_peer(k), :, lo:hi],
                dst_ref=rs_recv.at[k - 1, :, lo:hi],
                send_sem=rs.at[i, k - 1],
                recv_sem=rr.at[i, k - 1],
                device_id=(me, way_peer(k)),
                device_id_type=MESH,
            )
            copy.start()
            sums.append(copy)
    for copy in bc_copies:
        copy.wait_recv()
    both = bc_buf[0]
    for k in range(1, ways):
        both = both + bc_buf[k]
    bg_ref[...] = both[0]
    cg_ref[...] = both[1]
    for i, (lo, hi) in enumerate(CHUNKS):
        for copy in sums[i * (ways - 1) : (i + 1) * (ways - 1)]:
            copy.wait_recv()
        value = rs_send[tp, :, lo:hi].astype(F32)
        for k in range(ways - 1):
            value = value + rs_recv[k, :, lo:hi].astype(F32)
        out_ref[:, lo:hi] = value.astype(BF16)

    for copy in gathers + bc_copies + sums:
        copy.wait_send()
    wait_sets(fy_buf, ys, yr, True)
    wait_sets(t_buf, ts, tr, True)
    for sem in (fs, ps, ss):
        wait_row(sem)


def keep(*refs):
    half = len(refs) // 2
    sems = refs[-1]
    copies = [
        pltpu.make_async_copy(src, dst, sems.at[i])
        for i, (src, dst) in enumerate(zip(refs[:half], refs[half:-1]))
    ]
    for copy in copies:
        copy.start()
    for copy in copies:
        copy.wait()


def shards(
    layer_input,
    out_grad,
    w_in,
    w_gate,
    w_out,
    b_proj,
    c_proj,
    log_decay,
    d_skip,
    entry_state,
    doc_start,
):
    block, width = layer_input.shape
    channels = w_in.shape[0]
    state, tokens = b_proj.shape
    ways = lax.axis_size("tp")
    row_len = 8
    share = 2 * state // row_len
    groups = lax.axis_size("seq") // row_len
    tiles = -(-channels // LANES)
    anywhere = pl.BlockSpec(memory_space=pltpu.HBM)
    inside = pl.BlockSpec(memory_space=pltpu.VMEM)
    dma = pltpu.SemaphoreType.DMA
    results = pl.pallas_call(
        functools.partial(kernel, row_len, groups, SETS_Z, ways),
        out_shape=(
            pltpu.VMEM((block, width), BF16),
            pltpu.VMEM((state, tokens), F32),
            pltpu.VMEM((state, tokens), F32),
        ),
        in_specs=[anywhere] * 11,
        out_specs=(inside, inside, inside),
        scratch_shapes=[
            pltpu.VMEM((ways, block, width), BF16),
            pltpu.VMEM((ways, block, width), BF16),
            pltpu.VMEM((channels, width), BF16),
            pltpu.VMEM((channels, width), BF16),
            pltpu.VMEM((channels, width), BF16),
            pltpu.VMEM(b_proj.shape, BF16),
            pltpu.VMEM(c_proj.shape, BF16),
            pltpu.VMEM(log_decay.shape, BF16),
            pltpu.VMEM((1, channels), F32),
            pltpu.VMEM(entry_state.shape, F32),
            pltpu.VMEM((1, tokens), jnp.int32),
            pltpu.VMEM((state // share, tiles * share, LANES), F32),
            pltpu.VMEM((tiles * share, LANES), F32),
            pltpu.VMEM((row_len, tiles * share, LANES), F32),
            pltpu.VMEM((row_len, tiles * share, LANES), F32),
            pltpu.VMEM((groups, tiles * share, LANES), F32),
            pltpu.VMEM((row_len, tiles * share, LANES), F32),
            pltpu.VMEM((row_len, tiles * share, LANES), F32),
            pltpu.VMEM((row_len, tiles * share, LANES), F32),
            pltpu.VMEM((row_len, tiles * share, LANES), F32),
            pltpu.VMEM((groups, tiles * share, LANES), F32),
            pltpu.VMEM((2, state, tiles * LANES), F32),
            pltpu.VMEM((ways, 2, state, tokens), F32),
            pltpu.VMEM((tokens, width), F32),
            pltpu.VMEM((ways, block, width), BF16),
            pltpu.VMEM((ways - 1, block, width), BF16),
            pltpu.SemaphoreType.REGULAR,
            dma((11,)),
            dma((2, 6)),
            dma((2, 6)),
            dma,
            dma,
            dma((groups,)),
            dma((groups,)),
            dma,
            dma,
            dma((groups,)),
            dma((groups,)),
            dma,
            dma((row_len,)),
            dma((2, ways - 1)),
            dma((2, ways - 1)),
            dma((len(CHUNKS), ways - 1)),
            dma((len(CHUNKS), ways - 1)),
        ],
        compiler_params=pltpu.CompilerParams(
            collective_id=0, has_side_effects=True, vmem_limit_bytes=32 * 1024 * 1024
        ),
        name="gated_recurrence_backward",
    )(
        *(
            pltpu.with_memory_space_constraint(value, pltpu.HBM)
            for value in (
                layer_input,
                out_grad,
                w_in,
                w_gate,
                w_out,
                b_proj,
                c_proj,
                log_decay,
                d_skip.reshape(1, channels),
                entry_state,
                doc_start.reshape(1, tokens),
            )
        )
    )
    return pl.pallas_call(
        keep,
        out_shape=tuple(jax.ShapeDtypeStruct(r.shape, r.dtype) for r in results),
        in_specs=[inside] * 3,
        out_specs=(anywhere,) * 3,
        scratch_shapes=[dma((3,))],
        compiler_params=pltpu.CompilerParams(vmem_limit_bytes=2 * 1024 * 1024),
        name="results",
    )(*results)


def solution(mesh):
    in_specs = (
        P(("seq", "tp"), None),
        P(("seq", "tp"), None),
        P("tp", None),
        P("tp", None),
        P("tp", None),
        P(None, "seq"),
        P(None, "seq"),
        P(None, "seq"),
        P("tp"),
        P(None, "tp"),
        P("seq"),
    )
    out_specs = (P(("seq", "tp"), None), P(None, "seq"), P(None, "seq"))
    return jax.shard_map(shards, mesh=mesh, in_specs=in_specs, out_specs=out_specs, check_vma=False)
```

```python
import functools

import jax
import jax.numpy as jnp
from jax import lax
from jax.experimental import pallas as pl
from jax.experimental.pallas import tpu as pltpu
from jax.sharding import PartitionSpec as P

HDIM = 64
LANES = 128
SETS_Z = 4
MESH = pl.DeviceIdType.MESH
F32 = jnp.float32
BF16 = jnp.bfloat16
NN = (((1,), (0,)), ((), ()))
NT = (((1,), (1,)), ((), ()))
TN = (((0,), (0,)), ((), ()))
CHUNKS = ((0, 768), (768, 1600))


def dot(a, b, dims):
    return lax.dot_general(a, b, dims, preferred_element_type=F32)


def parts(value, count):
    high = value.astype(BF16)
    if count == 1:
        return (high,)
    return (high, (value - high.astype(F32)).astype(BF16))


def mm(a, b, dims):
    total = None
    for i, left in enumerate(a):
        for j, right in enumerate(b):
            if i + j < 2:
                term = dot(left, right, dims)
                total = term if total is None else total + term
    return total


def one_minus_exp(u):
    series = 1.0 - u / 6.0
    for k in (5.0, 4.0, 3.0, 2.0):
        series = 1.0 - u / k * series
    return jnp.where(u < 0.25, u * series, 1.0 - jnp.exp(-u))


def kernel(
    row_len,
    groups,
    sets_z,
    ways,
    x_hbm,
    g_hbm,
    wi_hbm,
    wg_hbm,
    wo_hbm,
    b_hbm,
    c_hbm,
    log_hbm,
    skip_hbm,
    entry_hbm,
    doc_hbm,
    out_ref,
    bg_ref,
    cg_ref,
    xbuf,
    gbuf,
    wi,
    wg,
    wo,
    b_ref,
    c_ref,
    log_ref,
    skip_ref,
    entry_ref,
    doc_ref,
    log_wide,
    entry_t,
    f_send,
    f_recv,
    f_pre,
    fy_buf,
    fy_wide,
    p_send,
    p_recv,
    res,
    land,
    t_buf,
    wide,
    bc_buf,
    from_gate,
    rs_send,
    rs_recv,
    heard,
    lsem,
    gs,
    gr,
    fs,
    fr,
    ys,
    yr,
    ps,
    pr,
    ts,
    tr,
    ss,
    sr,
    bs,
    br,
    rs,
    rr,
):
    me = lax.axis_index("seq")
    tp = lax.axis_index("tp")
    group = lax.div(me, row_len)
    rank = lax.rem(me, row_len)
    way = lax.rem(rank, 2)
    share = 2 * b_hbm.shape[0] // row_len
    block = x_hbm.shape[0]
    tokens = ways * block
    channels = wi_hbm.shape[0]
    heads = log_ref.shape[0]
    state = b_ref.shape[0]
    tiles = p_recv.shape[1] // share
    spans = [(k, k * LANES, min(channels, (k + 1) * LANES)) for k in range(tiles)]

    small = [
        pltpu.make_async_copy(src, dst, lsem.at[5 + i])
        for i, (src, dst) in enumerate(
            (
                (log_hbm, log_ref),
                (doc_hbm, doc_ref),
                (b_hbm, b_ref),
                (c_hbm, c_ref),
                (skip_hbm, skip_ref),
                (entry_hbm, entry_ref),
            )
        )
    ]
    local = [
        pltpu.make_async_copy(x_hbm, xbuf.at[tp], lsem.at[3]),
        pltpu.make_async_copy(g_hbm, gbuf.at[tp], lsem.at[4]),
        pltpu.make_async_copy(wi_hbm, wi, lsem.at[0]),
        pltpu.make_async_copy(wg_hbm, wg, lsem.at[1]),
        pltpu.make_async_copy(wo_hbm, wo, lsem.at[2]),
    ]
    for copy in local[:2] + small + local[2:]:
        copy.start()

    def row_peer(i):
        return group * row_len + lax.rem(rank + i, row_len)

    def way_peer(k):
        return lax.rem(tp + k, ways)

    line, spot = lax.div(group, sets_z), lax.rem(group, sets_z)
    lines = groups // sets_z
    last_line = lines - 1 - line

    def turn_of(place):
        return jnp.where(place < 2, place, 5 - place)

    turn = turn_of(spot)
    later = sets_z - 1 - turn

    def by_way(forward_value, backward_value):
        return forward_value * (1 - way) + backward_value * way

    def each_set(act):
        def step(i, carry):
            other_spot, other_line = lax.div(i, lines), lax.rem(i, lines)
            other = other_line * sets_z + other_spot
            gap = (other - group) * (1 - 2 * way)
            act(other, gap, turn_of(other_spot))
            return carry

        lax.fori_loop(0, groups, step, 0)

    def mirrored(place):
        return row_len - 2 - place + 2 * lax.rem(place, 2)

    def in_upper(place):
        return place >= sets_z // 2

    def share_of(member):
        return jnp.where(in_upper(spot), mirrored(member), member)

    mine = share_of(rank)

    def device_of(other):
        other_spot = lax.rem(other, sets_z)
        across = in_upper(spot) != in_upper(other_spot)
        return (other * row_len + jnp.where(across, mirrored(rank), rank), tp)

    barrier = pltpu.get_barrier_semaphore()

    def greet(i, carry):
        pl.semaphore_signal(barrier, inc=1, device_id=(row_peer(i), tp), device_id_type=MESH)
        return carry

    def greet_set(other, gap, other_turn):
        @pl.when(((gap < 0) & (turn <= other_turn)) | ((gap > 0) & (turn < other_turn)))
        def _():
            pl.semaphore_signal(barrier, inc=1, device_id=device_of(other), device_id_type=MESH)

    def answer_set(other, gap, other_turn):
        @pl.when((gap < 0) & (turn > other_turn))
        def _():
            pl.semaphore_signal(heard, inc=1, device_id=device_of(other), device_id_type=MESH)

    for k in range(1, ways):
        pl.semaphore_signal(barrier, inc=1, device_id=(me, way_peer(k)), device_id_type=MESH)
    lax.fori_loop(1, row_len, greet, 0)
    each_set(greet_set)
    before = by_way(last_line * (turn + 1) + line * turn, line * (turn + 1) + last_line * turn)
    before = before + jnp.where(spot == 2, 1, 0) + jnp.minimum(spot, 2)
    after = by_way(
        last_line * later + jnp.where(spot < 2, 3 - spot, 0),
        line * later + jnp.where(spot == 3, 1, 0),
    )
    pl.semaphore_wait(barrier, row_len + ways - 2 + before)

    half = block // 2
    right, left = way_peer(1), way_peer(ways - 1)
    gathers = []

    def pass_on(array, slot, part, to, landing):
        buf = (xbuf, gbuf)[array]
        where = buf.at[slot, pl.ds(part * half, half)]
        copy = pltpu.make_async_remote_copy(
            src_ref=where,
            dst_ref=where,
            send_sem=gs.at[array, landing],
            recv_sem=gr.at[array, landing],
            device_id=(me, to),
            device_id_type=MESH,
        )
        copy.start()
        gathers.append(copy)

    def landed(array, slot, part, landing):
        where = (xbuf, gbuf)[array].at[slot, pl.ds(part * half, half)]
        pltpu.make_async_copy(where, where, gr.at[array, landing]).wait()

    def forward(array):
        landed(array, left, 0, 0)
        pass_on(array, left, 0, right, 4)
        landed(array, right, 1, 3)
        pass_on(array, right, 1, left, 5)

    def gathered(array):
        landed(array, left, 1, 1)
        landed(array, right, 0, 2)
        landed(array, way_peer(2), 0, 4)
        landed(array, way_peer(2), 1, 5)

    def send_first(array):
        local[array].wait()
        pass_on(array, tp, 0, right, 0)
        pass_on(array, tp, 1, left, 3)

    def send_second(array):
        pass_on(array, tp, 1, right, 1)
        pass_on(array, tp, 0, left, 2)

    send_first(0)
    send_second(0)
    send_first(1)
    each_set(answer_set)

    def to_row(src_at, dst, send_sem, recv_sem):
        def send(i, carry):
            pltpu.make_async_remote_copy(
                src_ref=src_at(lax.rem(rank + i, row_len)),
                dst_ref=dst,
                send_sem=send_sem,
                recv_sem=recv_sem,
                device_id=(row_peer(i), tp),
                device_id_type=MESH,
            ).start()
            return carry

        lax.fori_loop(1, row_len, send, 0)

    def to_owners(side, src_at, dst, send_sem, recv_sem):
        def send(i, carry):
            peer = 2 * lax.rem(lax.div(rank, 2) + i, row_len // 2) + side

            @pl.when(peer != rank)
            def _():
                pltpu.make_async_remote_copy(
                    src_ref=src_at(peer),
                    dst_ref=dst,
                    send_sem=send_sem,
                    recv_sem=recv_sem,
                    device_id=(group * row_len + peer, tp),
                    device_id_type=MESH,
                ).start()

            return carry

        lax.fori_loop(0, row_len // 2, send, 0)

    def set_copy(buf, other, source, send_sem, recv_sem):
        return pltpu.make_async_remote_copy(
            src_ref=buf.at[source],
            dst_ref=buf.at[source],
            send_sem=send_sem.at[other],
            recv_sem=recv_sem.at[source],
            device_id=device_of(other),
            device_id_type=MESH,
        )

    def to_sets(buf, send_sem, recv_sem):
        def send(other, gap, other_turn):
            @pl.when(gap > 0)
            def _():
                set_copy(buf, other, group, send_sem, recv_sem).start()

        each_set(send)

    def wait_sets(buf, send_sem, recv_sem, sent):
        def wait(other, gap, other_turn):
            if sent:

                @pl.when(gap > 0)
                def _():
                    set_copy(buf, other, group, send_sem, recv_sem).wait_send()

            else:

                @pl.when(gap < 0)
                def _():
                    set_copy(buf, other, other, send_sem, recv_sem).wait_recv()

        each_set(wait)

    def wait_row(sem):
        every = p_recv.at[pl.ds(0, row_len - 1)]
        pltpu.make_async_copy(every, every, sem).wait()

    for copy in small:
        copy.wait()
    rows_of = log_wide.shape[0]
    head_row = lax.broadcasted_iota(jnp.int32, (rows_of, channels), 0)
    chan_row = lax.broadcasted_iota(jnp.int32, (rows_of, channels), 1) + tp * channels
    low = head_row * HDIM
    pick = jnp.where((chan_row >= low) & (chan_row < low + HDIM), 1.0, 0.0).astype(BF16)
    pick_all = jnp.concatenate([pick, pick, pick], axis=0)

    def to_channels(value):
        high = value.astype(BF16)
        rest = value - high.astype(F32)
        middle = rest.astype(BF16)
        lowest = (rest - middle.astype(F32)).astype(BF16)
        return dot(jnp.concatenate([high, middle, lowest], axis=0), pick_all, TN)

    log_wide[...] = jnp.zeros_like(log_wide)
    log_wide[0:heads, :] = log_ref[...].astype(F32)
    logs = log_wide[...]
    row_at = lax.broadcasted_iota(jnp.int32, (tokens, tokens), 0)
    col_at = lax.broadcasted_iota(jnp.int32, (tokens, tokens), 1)
    tri = jnp.where(row_at >= col_at, 1.0, 0.0).astype(BF16)
    at = lax.broadcasted_iota(jnp.int32, (1, tokens), 1) + me
    marks = jnp.where(at > 0, doc_ref[...], 0).astype(F32)
    marks_heads = jnp.broadcast_to(marks, logs.shape)
    cumulative = dot(logs.astype(BF16), tri, NT)
    counts = dot(marks_heads.astype(BF16), tri, NT)
    last = counts[:, tokens - 1 : tokens]
    total = cumulative[:, tokens - 1 : tokens]
    carry_in = to_channels(jnp.where(counts == 0.0, jnp.exp(cumulative), 0.0))
    factor = carry_in[tokens - 1 : tokens, :]

    f_send[...] = jnp.zeros_like(f_send)
    for k, lo, hi in spans:
        f_send[share * k : share * (k + 1), 0 : hi - lo] = jnp.broadcast_to(
            factor[:, lo:hi], (share, hi - lo)
        )
    f_recv[rank] = f_send[...]
    to_row(lambda peer: f_send, f_recv.at[rank], fs, fr)
    forward(0)
    send_second(1)

    p_send[...] = jnp.zeros_like(p_send)
    entry_t[...] = jnp.zeros_like(entry_t)

    def lay_out(rows, put):
        for q in range(state // share):
            for k, lo, hi in spans:
                put(q, slice(share * k, share * (k + 1)), slice(0, hi - lo), rows[share * q : share * (q + 1), lo:hi])

    def put_entry(q, rows, lanes, value):
        entry_t[q, rows, lanes] = value

    def put_state(q, rows, lanes, value):
        p_send[2 * q, rows, lanes] = value

    def put_grad(q, rows, lanes, value):
        p_send[2 * q + 1, rows, lanes] = value

    lay_out(entry_ref[...], put_entry)

    scales = to_channels(
        jnp.where(marks_heads == 1.0, 1.0, jnp.sqrt(one_minus_exp(-2.0 * logs)))
    )
    centre = cumulative[:, tokens // 2 : tokens // 2 + 1]
    rising = to_channels(jnp.exp(cumulative - centre))
    falling = to_channels(jnp.exp(centre - cumulative))
    carry_out = to_channels(jnp.where(counts == last, jnp.exp(total - cumulative), 0.0))
    marks_sq = jnp.broadcast_to(marks, (tokens, tokens)).astype(BF16)
    counts_col = dot(tri, marks_sq, NT)
    counts_row = dot(marks_sq, tri, NT)
    causal = (row_at >= col_at) & (counts_col == counts_row)
    b_rows = b_ref[...]
    c_rows = c_ref[...]
    crossed = jnp.where(causal, dot(c_rows, b_rows, TN), 0.0)
    skip = skip_ref[...]

    forward(1)

    wait_row(fr)

    def at_step(i, count):
        return jnp.where(way == 0, i, count - 1 - i)

    def decay_step(i, product):
        j = at_step(i, row_len)
        f_pre[j] = product
        return product * f_recv[j]

    product = lax.fori_loop(0, row_len, decay_step, jnp.ones(f_send.shape, F32), unroll=True)
    for k in range(tiles):
        fy_buf[group, k : k + 1, :] = product[share * k : share * k + 1, :]

    @pl.when(after == 0)
    def _():
        to_sets(fy_buf, ys, yr)


    gathered(0)
    local[2].wait()
    rows = xbuf[...].reshape(tokens, x_hbm.shape[1])
    pre_act = dot(rows, wi[...], NT)
    local[3].wait()
    gate_act = dot(rows, wg[...], NT)
    pre_sig = jax.nn.sigmoid(pre_act)
    gate_sig = jax.nn.sigmoid(gate_act)
    x_rows = (pre_act * pre_sig).astype(BF16).astype(F32)
    gate_silu = gate_act * gate_sig
    scaled = x_rows * scales
    scaled_out = parts(scaled * carry_out, 2)
    state_part = mm((b_rows,), scaled_out, NN)
    lay_out(state_part, put_state)
    to_owners(0, lambda peer: p_send.at[share_of(peer)], p_recv.at[rank], ps, pr)
    gathered(1)
    local[4].wait()
    mix_grad = dot(gbuf[...].reshape(tokens, g_hbm.shape[1]), wo[...], NT)
    y_grads = (mix_grad * gate_silu).astype(BF16).astype(F32)
    grads_in = parts(y_grads * carry_in, 2)
    grad_part = mm((c_rows,), grads_in, NN)
    lay_out(grad_part, put_grad)

    to_owners(1, lambda peer: p_send.at[share_of(peer)], p_recv.at[rank], ps, pr)
    p_recv[rank] = p_send[mine]

    @pl.when(after > 0)
    def _():
        pl.semaphore_wait(heard, after)
        to_sets(fy_buf, ys, yr)


    upper = parts(y_grads * rising, 2)
    lower = parts(scaled * falling, 2)
    weight = parts(jnp.where(causal, mm(upper, lower, NT), 0.0), 2)
    crossed_parts = parts(crossed, 2)
    ssm_own = rising * mm(crossed_parts, lower, NN) + skip * x_rows
    x_own = falling * mm(crossed_parts, upper, TN)
    c_own = mm((b_rows,), weight, NT)
    b_own = mm((c_rows,), weight, NN)
    pre_slope = pre_sig * (1.0 + pre_act * (1.0 - pre_sig))
    gate_slope = mix_grad * (gate_sig * (1.0 + gate_act * (1.0 - gate_sig)))

    wait_row(pr)

    def scan_step(i, carried):
        j = at_step(i, row_len)
        res[j] = carried
        return f_recv[j] * carried + p_recv[j]

    t_buf[group] = lax.fori_loop(0, row_len, scan_step, jnp.zeros(f_send.shape, F32), unroll=True)
    to_sets(t_buf, ts, tr)
    wait_sets(fy_buf, ys, yr, False)
    for k in range(tiles):
        fy_wide[:, share * k : share * (k + 1), :] = jnp.broadcast_to(
            fy_buf[:, k : k + 1, :], (groups, share, LANES)
        )
    wait_sets(t_buf, ts, tr, False)
    carried = jnp.where(way == 0, entry_t[lax.div(mine, 2)], 0.0)
    ahead = at_step(group, groups)
    for i in range(groups):
        j = at_step(i, groups)
        carried = jnp.where(i < ahead, fy_wide[j] * carried + t_buf[j], carried)
    res[...] = res[...] + f_pre[...] * carried[None]
    land[mine] = res[rank]
    to_row(lambda peer: res.at[peer], land.at[mine], ss, sr.at[mine])

    def carried_in(side):
        for q in range(state // share):
            owner = 2 * q + side

            @pl.when(owner != mine)
            def _():
                pltpu.make_async_copy(land.at[owner], land.at[owner], sr.at[owner]).wait()

            for k, lo, hi in spans:
                wide[side, share * q : share * (q + 1), lo : lo + LANES] = land[
                    owner, share * k : share * (k + 1), :
                ]
        return parts(wide[side, :, 0:channels], 2)

    bc_copies = []

    def share_out(side, value):
        bc_buf[tp, side] = value
        for k in range(1, ways):
            copy = pltpu.make_async_remote_copy(
                src_ref=bc_buf.at[tp, side],
                dst_ref=bc_buf.at[tp, side],
                send_sem=bs.at[side, k - 1],
                recv_sem=br.at[side, k - 1],
                device_id=(me, way_peer(k)),
                device_id_type=MESH,
            )
            copy.start()
            bc_copies.append(copy)

    state_in = carried_in(0)
    share_out(1, c_own + mm(state_in, grads_in, NT))
    ssm = (ssm_own + carry_in * mm((c_rows,), state_in, TN)).astype(BF16).astype(F32)
    gate_grad = (ssm * gate_slope).astype(BF16)
    from_gate[...] = dot(gate_grad, wg[...], NN)
    grad_in = carried_in(1)
    x_part = x_own + carry_out * mm((b_rows,), grad_in, TN)
    x_grad = (x_part * scales + skip * y_grads).astype(BF16).astype(F32)
    pre_grad = (x_grad * pre_slope).astype(BF16)
    order = (
        jnp.where(tp == 0, 3, jnp.where(tp == ways - 1, 1, 2)),
        jnp.where((tp == 0) | (tp == ways - 1), 2, 1),
        jnp.where(tp == 0, 1, 3),
    )
    sums = []
    for i, (lo, hi) in enumerate(CHUNKS):
        part = dot(pre_grad, wi[:, lo:hi], NN) + from_gate[:, lo:hi]
        rs_send[:, :, lo:hi] = part.reshape(ways, block, hi - lo).astype(BF16)
        for k in order:
            copy = pltpu.make_async_remote_copy(
                src_ref=rs_send.at[way_peer(k), :, lo:hi],
                dst_ref=rs_recv.at[k - 1, :, lo:hi],
                send_sem=rs.at[i, k - 1],
                recv_sem=rr.at[i, k - 1],
                device_id=(me, way_peer(k)),
                device_id_type=MESH,
            )
            copy.start()
            sums.append(copy)
    share_out(0, b_own + mm(grad_in, scaled_out, NT))
    for copy in bc_copies:
        copy.wait_recv()
    both = bc_buf[0]
    for k in range(1, ways):
        both = both + bc_buf[k]
    bg_ref[...] = both[0]
    cg_ref[...] = both[1]
    for i, (lo, hi) in enumerate(CHUNKS):
        for copy in sums[i * (ways - 1) : (i + 1) * (ways - 1)]:
            copy.wait_recv()
        value = rs_send[tp, :, lo:hi].astype(F32)
        for k in range(ways - 1):
            value = value + rs_recv[k, :, lo:hi].astype(F32)
        out_ref[:, lo:hi] = value.astype(BF16)

    for copy in gathers + bc_copies + sums:
        copy.wait_send()
    wait_sets(fy_buf, ys, yr, True)
    wait_sets(t_buf, ts, tr, True)
    for sem in (fs, ps, ss):
        wait_row(sem)


def keep(*refs):
    half = len(refs) // 2
    sems = refs[-1]
    copies = [
        pltpu.make_async_copy(src, dst, sems.at[i])
        for i, (src, dst) in enumerate(zip(refs[:half], refs[half:-1]))
    ]
    for copy in copies:
        copy.start()
    for copy in copies:
        copy.wait()


def shards(
    layer_input,
    out_grad,
    w_in,
    w_gate,
    w_out,
    b_proj,
    c_proj,
    log_decay,
    d_skip,
    entry_state,
    doc_start,
):
    block, width = layer_input.shape
    channels = w_in.shape[0]
    state, tokens = b_proj.shape
    ways = lax.axis_size("tp")
    row_len = 8
    share = 2 * state // row_len
    groups = lax.axis_size("seq") // row_len
    tiles = -(-channels // LANES)
    anywhere = pl.BlockSpec(memory_space=pltpu.HBM)
    inside = pl.BlockSpec(memory_space=pltpu.VMEM)
    dma = pltpu.SemaphoreType.DMA
    results = pl.pallas_call(
        functools.partial(kernel, row_len, groups, SETS_Z, ways),
        out_shape=(
            pltpu.VMEM((block, width), BF16),
            pltpu.VMEM((state, tokens), F32),
            pltpu.VMEM((state, tokens), F32),
        ),
        in_specs=[anywhere] * 11,
        out_specs=(inside, inside, inside),
        scratch_shapes=[
            pltpu.VMEM((ways, block, width), BF16),
            pltpu.VMEM((ways, block, width), BF16),
            pltpu.VMEM((channels, width), BF16),
            pltpu.VMEM((channels, width), BF16),
            pltpu.VMEM((channels, width), BF16),
            pltpu.VMEM(b_proj.shape, BF16),
            pltpu.VMEM(c_proj.shape, BF16),
            pltpu.VMEM(log_decay.shape, BF16),
            pltpu.VMEM((1, channels), F32),
            pltpu.VMEM(entry_state.shape, F32),
            pltpu.VMEM((1, tokens), jnp.int32),
            pltpu.VMEM((-(-log_decay.shape[0] // 16) * 16, tokens), F32),
            pltpu.VMEM((state // share, tiles * share, LANES), F32),
            pltpu.VMEM((tiles * share, LANES), F32),
            pltpu.VMEM((row_len, tiles * share, LANES), F32),
            pltpu.VMEM((row_len, tiles * share, LANES), F32),
            pltpu.VMEM((groups, tiles, LANES), F32),
            pltpu.VMEM((groups, tiles * share, LANES), F32),
            pltpu.VMEM((row_len, tiles * share, LANES), F32),
            pltpu.VMEM((row_len, tiles * share, LANES), F32),
            pltpu.VMEM((row_len, tiles * share, LANES), F32),
            pltpu.VMEM((row_len, tiles * share, LANES), F32),
            pltpu.VMEM((groups, tiles * share, LANES), F32),
            pltpu.VMEM((2, state, tiles * LANES), F32),
            pltpu.VMEM((ways, 2, state, tokens), F32),
            pltpu.VMEM((tokens, width), F32),
            pltpu.VMEM((ways, block, width), BF16),
            pltpu.VMEM((ways - 1, block, width), BF16),
            pltpu.SemaphoreType.REGULAR,
            dma((11,)),
            dma((2, 6)),
            dma((2, 6)),
            dma,
            dma,
            dma((groups,)),
            dma((groups,)),
            dma,
            dma,
            dma((groups,)),
            dma((groups,)),
            dma,
            dma((row_len,)),
            dma((2, ways - 1)),
            dma((2, ways - 1)),
            dma((len(CHUNKS), ways - 1)),
            dma((len(CHUNKS), ways - 1)),
        ],
        compiler_params=pltpu.CompilerParams(
            collective_id=0, has_side_effects=True, vmem_limit_bytes=32 * 1024 * 1024
        ),
        name="gated_recurrence_backward",
    )(
        *(
            pltpu.with_memory_space_constraint(value, pltpu.HBM)
            for value in (
                layer_input,
                out_grad,
                w_in,
                w_gate,
                w_out,
                b_proj,
                c_proj,
                log_decay,
                d_skip.reshape(1, channels),
                entry_state,
                doc_start.reshape(1, tokens),
            )
        )
    )
    return pl.pallas_call(
        keep,
        out_shape=tuple(jax.ShapeDtypeStruct(r.shape, r.dtype) for r in results),
        in_specs=[inside] * 3,
        out_specs=(anywhere,) * 3,
        scratch_shapes=[dma((3,))],
        compiler_params=pltpu.CompilerParams(vmem_limit_bytes=2 * 1024 * 1024),
        name="results",
    )(*results)


def solution(mesh):
    in_specs = (
        P(("seq", "tp"), None),
        P(("seq", "tp"), None),
        P("tp", None),
        P("tp", None),
        P("tp", None),
        P(None, "seq"),
        P(None, "seq"),
        P(None, "seq"),
        P("tp"),
        P(None, "tp"),
        P("seq"),
    )
    out_specs = (P(("seq", "tp"), None), P(None, "seq"), P(None, "seq"))
    return jax.shard_map(shards, mesh=mesh, in_specs=in_specs, out_specs=out_specs, check_vma=False)
```

```python
import functools

import jax
import jax.numpy as jnp
from jax import lax
from jax.experimental import pallas as pl
from jax.experimental.pallas import tpu as pltpu
from jax.sharding import PartitionSpec as P

HDIM = 64
LANES = 128
SETS_Z = 4
MESH = pl.DeviceIdType.MESH
F32 = jnp.float32
BF16 = jnp.bfloat16
NN = (((1,), (0,)), ((), ()))
NT = (((1,), (1,)), ((), ()))
TN = (((0,), (0,)), ((), ()))
CHUNKS = ((0, 768), (768, 1600))


def dot(a, b, dims):
    return lax.dot_general(a, b, dims, preferred_element_type=F32)


def parts(value, count):
    high = value.astype(BF16)
    if count == 1:
        return (high,)
    return (high, (value - high.astype(F32)).astype(BF16))


def mm(a, b, dims):
    total = None
    for i, left in enumerate(a):
        for j, right in enumerate(b):
            if i + j < 2:
                term = dot(left, right, dims)
                total = term if total is None else total + term
    return total


def one_minus_exp(u):
    series = 1.0 - u / 6.0
    for k in (5.0, 4.0, 3.0, 2.0):
        series = 1.0 - u / k * series
    return jnp.where(u < 0.25, u * series, 1.0 - jnp.exp(-u))


def kernel(
    row_len,
    groups,
    sets_z,
    ways,
    x_hbm,
    g_hbm,
    wi_hbm,
    wg_hbm,
    wo_hbm,
    b_hbm,
    c_hbm,
    log_hbm,
    skip_hbm,
    entry_hbm,
    doc_hbm,
    out_ref,
    bg_ref,
    cg_ref,
    xbuf,
    gbuf,
    wi,
    wg,
    wo,
    b_ref,
    c_ref,
    log_ref,
    skip_ref,
    entry_ref,
    doc_ref,
    log_wide,
    entry_t,
    f_send,
    f_recv,
    f_pre,
    fy_buf,
    fy_wide,
    p_send,
    p_recv,
    res,
    land,
    t_buf,
    wide,
    bc_buf,
    from_gate,
    rs_send,
    rs_recv,
    heard,
    lsem,
    gs,
    gr,
    fs,
    fr,
    ys,
    yr,
    ps,
    pr,
    ts,
    tr,
    ss,
    sr,
    bs,
    br,
    rs,
    rr,
):
    me = lax.axis_index("seq")
    tp = lax.axis_index("tp")
    group = lax.div(me, row_len)
    rank = lax.rem(me, row_len)
    way = lax.rem(rank, 2)
    share = 2 * b_hbm.shape[0] // row_len
    block = x_hbm.shape[0]
    tokens = ways * block
    channels = wi_hbm.shape[0]
    heads = log_ref.shape[0]
    state = b_ref.shape[0]
    tiles = p_recv.shape[1] // share
    spans = [(k, k * LANES, min(channels, (k + 1) * LANES)) for k in range(tiles)]

    small = [
        pltpu.make_async_copy(src, dst, lsem.at[5 + i])
        for i, (src, dst) in enumerate(
            (
                (log_hbm, log_ref),
                (doc_hbm, doc_ref),
                (b_hbm, b_ref),
                (c_hbm, c_ref),
                (skip_hbm, skip_ref),
                (entry_hbm, entry_ref),
            )
        )
    ]
    local = [
        pltpu.make_async_copy(x_hbm, xbuf.at[tp], lsem.at[3]),
        pltpu.make_async_copy(g_hbm, gbuf.at[tp], lsem.at[4]),
        pltpu.make_async_copy(wi_hbm, wi, lsem.at[0]),
        pltpu.make_async_copy(wg_hbm, wg, lsem.at[1]),
        pltpu.make_async_copy(wo_hbm, wo, lsem.at[2]),
    ]
    for copy in local[:2] + small + local[2:]:
        copy.start()

    def row_peer(i):
        return group * row_len + lax.rem(rank + i, row_len)

    def way_peer(k):
        return lax.rem(tp + k, ways)

    line, spot = lax.div(group, sets_z), lax.rem(group, sets_z)
    lines = groups // sets_z
    last_line = lines - 1 - line

    def turn_of(place):
        return jnp.where(place < 2, place, 5 - place)

    turn = turn_of(spot)
    later = sets_z - 1 - turn

    def by_way(forward_value, backward_value):
        return forward_value * (1 - way) + backward_value * way

    def each_set(act):
        def step(i, carry):
            other_spot, other_line = lax.div(i, lines), lax.rem(i, lines)
            other = other_line * sets_z + other_spot
            gap = (other - group) * (1 - 2 * way)
            act(other, gap, turn_of(other_spot))
            return carry

        lax.fori_loop(0, groups, step, 0, unroll=True)

    def mirrored(place):
        return row_len - 2 - place + 2 * lax.rem(place, 2)

    def in_upper(place):
        return place >= sets_z // 2

    def share_of(member):
        return jnp.where(in_upper(spot), mirrored(member), member)

    mine = share_of(rank)

    def device_of(other):
        other_spot = lax.rem(other, sets_z)
        across = in_upper(spot) != in_upper(other_spot)
        return (other * row_len + jnp.where(across, mirrored(rank), rank), tp)

    barrier = pltpu.get_barrier_semaphore()

    def greet(i, carry):
        pl.semaphore_signal(barrier, inc=1, device_id=(row_peer(i), tp), device_id_type=MESH)
        return carry

    def greet_set(other, gap, other_turn):
        @pl.when(((gap < 0) & (turn <= other_turn)) | ((gap > 0) & (turn < other_turn)))
        def _():
            pl.semaphore_signal(barrier, inc=1, device_id=device_of(other), device_id_type=MESH)

    def answer_set(other, gap, other_turn):
        @pl.when((gap < 0) & (turn > other_turn))
        def _():
            pl.semaphore_signal(heard, inc=1, device_id=device_of(other), device_id_type=MESH)

    for k in range(1, ways):
        pl.semaphore_signal(barrier, inc=1, device_id=(me, way_peer(k)), device_id_type=MESH)
    lax.fori_loop(1, row_len, greet, 0)
    each_set(greet_set)
    before = by_way(last_line * (turn + 1) + line * turn, line * (turn + 1) + last_line * turn)
    before = before + jnp.where(spot == 2, 1, 0) + jnp.minimum(spot, 2)
    after = by_way(
        last_line * later + jnp.where(spot < 2, 3 - spot, 0),
        line * later + jnp.where(spot == 3, 1, 0),
    )
    pl.semaphore_wait(barrier, row_len + ways - 2 + before)

    half = block // 2
    right, left = way_peer(1), way_peer(ways - 1)
    gathers = []

    def pass_on(array, slot, part, to, landing):
        buf = (xbuf, gbuf)[array]
        where = buf.at[slot, pl.ds(part * half, half)]
        copy = pltpu.make_async_remote_copy(
            src_ref=where,
            dst_ref=where,
            send_sem=gs.at[array, landing],
            recv_sem=gr.at[array, landing],
            device_id=(me, to),
            device_id_type=MESH,
        )
        copy.start()
        gathers.append(copy)

    def landed(array, slot, part, landing):
        where = (xbuf, gbuf)[array].at[slot, pl.ds(part * half, half)]
        pltpu.make_async_copy(where, where, gr.at[array, landing]).wait()

    def forward(array):
        landed(array, left, 0, 0)
        pass_on(array, left, 0, right, 4)
        landed(array, right, 1, 3)
        pass_on(array, right, 1, left, 5)

    def gathered(array):
        landed(array, left, 1, 1)
        landed(array, right, 0, 2)
        landed(array, way_peer(2), 0, 4)
        landed(array, way_peer(2), 1, 5)

    def send_first(array):
        local[array].wait()
        pass_on(array, tp, 0, right, 0)
        pass_on(array, tp, 1, left, 3)

    def send_second(array):
        pass_on(array, tp, 1, right, 1)
        pass_on(array, tp, 0, left, 2)

    send_first(0)
    send_second(0)
    send_first(1)
    each_set(answer_set)

    def to_row(src_at, dst, send_sem, recv_sem):
        def send(i, carry):
            pltpu.make_async_remote_copy(
                src_ref=src_at(lax.rem(rank + i, row_len)),
                dst_ref=dst,
                send_sem=send_sem,
                recv_sem=recv_sem,
                device_id=(row_peer(i), tp),
                device_id_type=MESH,
            ).start()
            return carry

        lax.fori_loop(1, row_len, send, 0)

    def to_owners(side, src_at, dst, send_sem, recv_sem):
        def send(i, carry):
            peer = 2 * lax.rem(lax.div(rank, 2) + i, row_len // 2) + side

            @pl.when(peer != rank)
            def _():
                pltpu.make_async_remote_copy(
                    src_ref=src_at(peer),
                    dst_ref=dst,
                    send_sem=send_sem,
                    recv_sem=recv_sem,
                    device_id=(group * row_len + peer, tp),
                    device_id_type=MESH,
                ).start()

            return carry

        lax.fori_loop(0, row_len // 2, send, 0)

    def set_copy(buf, other, source, send_sem, recv_sem):
        return pltpu.make_async_remote_copy(
            src_ref=buf.at[source],
            dst_ref=buf.at[source],
            send_sem=send_sem.at[other],
            recv_sem=recv_sem.at[source],
            device_id=device_of(other),
            device_id_type=MESH,
        )

    def to_sets(buf, send_sem, recv_sem):
        def send(other, gap, other_turn):
            @pl.when(gap > 0)
            def _():
                set_copy(buf, other, group, send_sem, recv_sem).start()

        each_set(send)

    def wait_sets(buf, send_sem, recv_sem, sent):
        def wait(other, gap, other_turn):
            if sent:

                @pl.when(gap > 0)
                def _():
                    set_copy(buf, other, group, send_sem, recv_sem).wait_send()

            else:

                @pl.when(gap < 0)
                def _():
                    set_copy(buf, other, other, send_sem, recv_sem).wait_recv()

        each_set(wait)

    def wait_row(sem):
        every = p_recv.at[pl.ds(0, row_len - 1)]
        pltpu.make_async_copy(every, every, sem).wait()

    for copy in small:
        copy.wait()
    rows_of = log_wide.shape[0]
    head_row = lax.broadcasted_iota(jnp.int32, (rows_of, channels), 0)
    chan_row = lax.broadcasted_iota(jnp.int32, (rows_of, channels), 1) + tp * channels
    low = head_row * HDIM
    pick = jnp.where((chan_row >= low) & (chan_row < low + HDIM), 1.0, 0.0).astype(BF16)
    pick_all = jnp.concatenate([pick, pick, pick], axis=0)

    def to_channels(value):
        high = value.astype(BF16)
        rest = value - high.astype(F32)
        middle = rest.astype(BF16)
        lowest = (rest - middle.astype(F32)).astype(BF16)
        return dot(jnp.concatenate([high, middle, lowest], axis=0), pick_all, TN)

    log_wide[...] = jnp.zeros_like(log_wide)
    log_wide[0:heads, :] = log_ref[...].astype(F32)
    logs = log_wide[...]
    row_at = lax.broadcasted_iota(jnp.int32, (tokens, tokens), 0)
    col_at = lax.broadcasted_iota(jnp.int32, (tokens, tokens), 1)
    tri = jnp.where(row_at >= col_at, 1.0, 0.0).astype(BF16)
    at = lax.broadcasted_iota(jnp.int32, (1, tokens), 1) + me
    marks = jnp.where(at > 0, doc_ref[...], 0).astype(F32)
    marks_heads = jnp.broadcast_to(marks, logs.shape)
    cumulative = dot(logs.astype(BF16), tri, NT)
    counts = dot(marks_heads.astype(BF16), tri, NT)
    last = counts[:, tokens - 1 : tokens]
    total = cumulative[:, tokens - 1 : tokens]
    carry_in = to_channels(jnp.where(counts == 0.0, jnp.exp(cumulative), 0.0))
    factor = carry_in[tokens - 1 : tokens, :]

    f_send[...] = jnp.zeros_like(f_send)
    for k, lo, hi in spans:
        f_send[share * k : share * (k + 1), 0 : hi - lo] = jnp.broadcast_to(
            factor[:, lo:hi], (share, hi - lo)
        )
    f_recv[rank] = f_send[...]
    to_row(lambda peer: f_send, f_recv.at[rank], fs, fr)
    forward(0)
    send_second(1)

    p_send[...] = jnp.zeros_like(p_send)
    entry_t[...] = jnp.zeros_like(entry_t)

    def lay_out(rows, put):
        for q in range(state // share):
            for k, lo, hi in spans:
                put(q, slice(share * k, share * (k + 1)), slice(0, hi - lo), rows[share * q : share * (q + 1), lo:hi])

    def put_entry(q, rows, lanes, value):
        entry_t[q, rows, lanes] = value

    def put_state(q, rows, lanes, value):
        p_send[2 * q, rows, lanes] = value

    def put_grad(q, rows, lanes, value):
        p_send[2 * q + 1, rows, lanes] = value

    lay_out(entry_ref[...], put_entry)

    scales = to_channels(
        jnp.where(marks_heads == 1.0, 1.0, jnp.sqrt(one_minus_exp(-2.0 * logs)))
    )
    centre = cumulative[:, tokens // 2 : tokens // 2 + 1]
    rising = to_channels(jnp.exp(cumulative - centre))
    falling = to_channels(jnp.exp(centre - cumulative))
    carry_out = to_channels(jnp.where(counts == last, jnp.exp(total - cumulative), 0.0))
    marks_sq = jnp.broadcast_to(marks, (tokens, tokens)).astype(BF16)
    counts_col = dot(tri, marks_sq, NT)
    counts_row = dot(marks_sq, tri, NT)
    causal = (row_at >= col_at) & (counts_col == counts_row)
    b_rows = b_ref[...]
    c_rows = c_ref[...]
    crossed = jnp.where(causal, dot(c_rows, b_rows, TN), 0.0)
    skip = skip_ref[...]

    forward(1)

    wait_row(fr)

    def at_step(i, count):
        return jnp.where(way == 0, i, count - 1 - i)

    def decay_step(i, product):
        j = at_step(i, row_len)
        f_pre[j] = product
        return product * f_recv[j]

    product = lax.fori_loop(0, row_len, decay_step, jnp.ones(f_send.shape, F32), unroll=True)
    for k in range(tiles):
        fy_buf[group, k : k + 1, :] = product[share * k : share * k + 1, :]

    @pl.when(after == 0)
    def _():
        to_sets(fy_buf, ys, yr)


    gathered(0)
    local[2].wait()
    rows = xbuf[...].reshape(tokens, x_hbm.shape[1])
    pre_act = dot(rows, wi[...], NT)
    local[3].wait()
    gate_act = dot(rows, wg[...], NT)
    pre_sig = jax.nn.sigmoid(pre_act)
    gate_sig = jax.nn.sigmoid(gate_act)
    x_rows = (pre_act * pre_sig).astype(BF16).astype(F32)
    gate_silu = gate_act * gate_sig
    scaled = x_rows * scales
    scaled_out = parts(scaled * carry_out, 2)
    state_part = mm((b_rows,), scaled_out, NN)
    lay_out(state_part, put_state)
    to_owners(0, lambda peer: p_send.at[share_of(peer)], p_recv.at[rank], ps, pr)
    gathered(1)
    local[4].wait()
    mix_grad = dot(gbuf[...].reshape(tokens, g_hbm.shape[1]), wo[...], NT)
    y_grads = (mix_grad * gate_silu).astype(BF16).astype(F32)
    grads_in = parts(y_grads * carry_in, 2)
    grad_part = mm((c_rows,), grads_in, NN)
    lay_out(grad_part, put_grad)

    to_owners(1, lambda peer: p_send.at[share_of(peer)], p_recv.at[rank], ps, pr)
    p_recv[rank] = p_send[mine]

    @pl.when(after > 0)
    def _():
        pl.semaphore_wait(heard, after)
        to_sets(fy_buf, ys, yr)


    upper = parts(y_grads * rising, 2)
    lower = parts(scaled * falling, 2)
    weight = parts(jnp.where(causal, mm(upper, lower, NT), 0.0), 2)
    crossed_parts = parts(crossed, 2)
    ssm_own = rising * mm(crossed_parts, lower, NN) + skip * x_rows
    x_own = falling * mm(crossed_parts, upper, TN)
    c_own = mm((b_rows,), weight, NT)
    b_own = mm((c_rows,), weight, NN)
    pre_slope = pre_sig * (1.0 + pre_act * (1.0 - pre_sig))
    gate_slope = mix_grad * (gate_sig * (1.0 + gate_act * (1.0 - gate_sig)))

    wait_row(pr)

    def scan_step(i, carried):
        j = at_step(i, row_len)
        res[j] = carried
        return f_recv[j] * carried + p_recv[j]

    t_buf[group] = lax.fori_loop(0, row_len, scan_step, jnp.zeros(f_send.shape, F32), unroll=True)
    to_sets(t_buf, ts, tr)
    wait_sets(fy_buf, ys, yr, False)
    for k in range(tiles):
        fy_wide[:, share * k : share * (k + 1), :] = jnp.broadcast_to(
            fy_buf[:, k : k + 1, :], (groups, share, LANES)
        )
    wait_sets(t_buf, ts, tr, False)
    carried = jnp.where(way == 0, entry_t[lax.div(mine, 2)], 0.0)
    ahead = at_step(group, groups)
    for i in range(groups):
        j = at_step(i, groups)
        carried = jnp.where(i < ahead, fy_wide[j] * carried + t_buf[j], carried)
    res[...] = res[...] + f_pre[...] * carried[None]
    land[mine] = res[rank]
    to_row(lambda peer: res.at[peer], land.at[mine], ss, sr.at[mine])

    def carried_in(side):
        for q in range(state // share):
            owner = 2 * q + side

            @pl.when(owner != mine)
            def _():
                pltpu.make_async_copy(land.at[owner], land.at[owner], sr.at[owner]).wait()

            for k, lo, hi in spans:
                wide[side, share * q : share * (q + 1), lo : lo + LANES] = land[
                    owner, share * k : share * (k + 1), :
                ]
        return parts(wide[side, :, 0:channels], 2)

    bc_copies = []

    def share_out(side, value):
        bc_buf[tp, side] = value
        for k in range(1, ways):
            copy = pltpu.make_async_remote_copy(
                src_ref=bc_buf.at[tp, side],
                dst_ref=bc_buf.at[tp, side],
                send_sem=bs.at[side, k - 1],
                recv_sem=br.at[side, k - 1],
                device_id=(me, way_peer(k)),
                device_id_type=MESH,
            )
            copy.start()
            bc_copies.append(copy)

    state_in = carried_in(0)
    share_out(1, c_own + mm(state_in, grads_in, NT))
    ssm = (ssm_own + carry_in * mm((c_rows,), state_in, TN)).astype(BF16).astype(F32)
    gate_grad = (ssm * gate_slope).astype(BF16)
    from_gate[...] = dot(gate_grad, wg[...], NN)
    grad_in = carried_in(1)
    x_part = x_own + carry_out * mm((b_rows,), grad_in, TN)
    x_grad = (x_part * scales + skip * y_grads).astype(BF16).astype(F32)
    pre_grad = (x_grad * pre_slope).astype(BF16)
    order = (
        jnp.where(tp == 0, 3, jnp.where(tp == ways - 1, 1, 2)),
        jnp.where((tp == 0) | (tp == ways - 1), 2, 1),
        jnp.where(tp == 0, 1, 3),
    )
    sums = []
    for i, (lo, hi) in enumerate(CHUNKS):
        part = dot(pre_grad, wi[:, lo:hi], NN) + from_gate[:, lo:hi]
        rs_send[:, :, lo:hi] = part.reshape(ways, block, hi - lo).astype(BF16)
        for k in order:
            copy = pltpu.make_async_remote_copy(
                src_ref=rs_send.at[way_peer(k), :, lo:hi],
                dst_ref=rs_recv.at[k - 1, :, lo:hi],
                send_sem=rs.at[i, k - 1],
                recv_sem=rr.at[i, k - 1],
                device_id=(me, way_peer(k)),
                device_id_type=MESH,
            )
            copy.start()
            sums.append(copy)
    share_out(0, b_own + mm(grad_in, scaled_out, NT))
    for copy in bc_copies:
        copy.wait_recv()
    both = bc_buf[0]
    for k in range(1, ways):
        both = both + bc_buf[k]
    bg_ref[...] = both[0]
    cg_ref[...] = both[1]
    for i, (lo, hi) in enumerate(CHUNKS):
        for copy in sums[i * (ways - 1) : (i + 1) * (ways - 1)]:
            copy.wait_recv()
        value = rs_send[tp, :, lo:hi].astype(F32)
        for k in range(ways - 1):
            value = value + rs_recv[k, :, lo:hi].astype(F32)
        out_ref[:, lo:hi] = value.astype(BF16)

    for copy in gathers + bc_copies + sums:
        copy.wait_send()
    wait_sets(fy_buf, ys, yr, True)
    wait_sets(t_buf, ts, tr, True)
    for sem in (fs, ps, ss):
        wait_row(sem)


def keep(*refs):
    half = len(refs) // 2
    sems = refs[-1]
    copies = [
        pltpu.make_async_copy(src, dst, sems.at[i])
        for i, (src, dst) in enumerate(zip(refs[:half], refs[half:-1]))
    ]
    for copy in copies:
        copy.start()
    for copy in copies:
        copy.wait()


def shards(
    layer_input,
    out_grad,
    w_in,
    w_gate,
    w_out,
    b_proj,
    c_proj,
    log_decay,
    d_skip,
    entry_state,
    doc_start,
):
    block, width = layer_input.shape
    channels = w_in.shape[0]
    state, tokens = b_proj.shape
    ways = lax.axis_size("tp")
    row_len = 8
    share = 2 * state // row_len
    groups = lax.axis_size("seq") // row_len
    tiles = -(-channels // LANES)
    anywhere = pl.BlockSpec(memory_space=pltpu.HBM)
    inside = pl.BlockSpec(memory_space=pltpu.VMEM)
    dma = pltpu.SemaphoreType.DMA
    results = pl.pallas_call(
        functools.partial(kernel, row_len, groups, SETS_Z, ways),
        out_shape=(
            pltpu.VMEM((block, width), BF16),
            pltpu.VMEM((state, tokens), F32),
            pltpu.VMEM((state, tokens), F32),
        ),
        in_specs=[anywhere] * 11,
        out_specs=(inside, inside, inside),
        scratch_shapes=[
            pltpu.VMEM((ways, block, width), BF16),
            pltpu.VMEM((ways, block, width), BF16),
            pltpu.VMEM((channels, width), BF16),
            pltpu.VMEM((channels, width), BF16),
            pltpu.VMEM((channels, width), BF16),
            pltpu.VMEM(b_proj.shape, BF16),
            pltpu.VMEM(c_proj.shape, BF16),
            pltpu.VMEM(log_decay.shape, BF16),
            pltpu.VMEM((1, channels), F32),
            pltpu.VMEM(entry_state.shape, F32),
            pltpu.VMEM((1, tokens), jnp.int32),
            pltpu.VMEM((-(-log_decay.shape[0] // 16) * 16, tokens), F32),
            pltpu.VMEM((state // share, tiles * share, LANES), F32),
            pltpu.VMEM((tiles * share, LANES), F32),
            pltpu.VMEM((row_len, tiles * share, LANES), F32),
            pltpu.VMEM((row_len, tiles * share, LANES), F32),
            pltpu.VMEM((groups, tiles, LANES), F32),
            pltpu.VMEM((groups, tiles * share, LANES), F32),
            pltpu.VMEM((row_len, tiles * share, LANES), F32),
            pltpu.VMEM((row_len, tiles * share, LANES), F32),
            pltpu.VMEM((row_len, tiles * share, LANES), F32),
            pltpu.VMEM((row_len, tiles * share, LANES), F32),
            pltpu.VMEM((groups, tiles * share, LANES), F32),
            pltpu.VMEM((2, state, tiles * LANES), F32),
            pltpu.VMEM((ways, 2, state, tokens), F32),
            pltpu.VMEM((tokens, width), F32),
            pltpu.VMEM((ways, block, width), BF16),
            pltpu.VMEM((ways - 1, block, width), BF16),
            pltpu.SemaphoreType.REGULAR,
            dma((11,)),
            dma((2, 6)),
            dma((2, 6)),
            dma,
            dma,
            dma((groups,)),
            dma((groups,)),
            dma,
            dma,
            dma((groups,)),
            dma((groups,)),
            dma,
            dma((row_len,)),
            dma((2, ways - 1)),
            dma((2, ways - 1)),
            dma((len(CHUNKS), ways - 1)),
            dma((len(CHUNKS), ways - 1)),
        ],
        compiler_params=pltpu.CompilerParams(
            collective_id=0, has_side_effects=True, vmem_limit_bytes=32 * 1024 * 1024
        ),
        name="gated_recurrence_backward",
    )(
        *(
            pltpu.with_memory_space_constraint(value, pltpu.HBM)
            for value in (
                layer_input,
                out_grad,
                w_in,
                w_gate,
                w_out,
                b_proj,
                c_proj,
                log_decay,
                d_skip.reshape(1, channels),
                entry_state,
                doc_start.reshape(1, tokens),
            )
        )
    )
    return pl.pallas_call(
        keep,
        out_shape=tuple(jax.ShapeDtypeStruct(r.shape, r.dtype) for r in results),
        in_specs=[inside] * 3,
        out_specs=(anywhere,) * 3,
        scratch_shapes=[dma((3,))],
        compiler_params=pltpu.CompilerParams(vmem_limit_bytes=2 * 1024 * 1024),
        name="results",
    )(*results)


def solution(mesh):
    in_specs = (
        P(("seq", "tp"), None),
        P(("seq", "tp"), None),
        P("tp", None),
        P("tp", None),
        P("tp", None),
        P(None, "seq"),
        P(None, "seq"),
        P(None, "seq"),
        P("tp"),
        P(None, "tp"),
        P("seq"),
    )
    out_specs = (P(("seq", "tp"), None), P(None, "seq"), P(None, "seq"))
    return jax.shard_map(shards, mesh=mesh, in_specs=in_specs, out_specs=out_specs, check_vma=False)
```
